128 devices in a mesh: gy: 16 (over x, z_lo, core), gz: 8 (over y, z_hi).
Axes of the slice: x: 4, y: 4, z: 4 (z_hi: 2, z_lo: 2; z = z_hi * 2 + z_lo), core: 2. Of those that a mesh axis runs over, the one named last changes fastest.
Arguments:
- velocity: float32 [3, 128, 512, 1024], P(None, None, 'gy', 'gz'), may hold values from -8 to 8
- wall_mask: int32 [512, 1024], P('gy', 'gz'), may hold values 0 or 1
- hartmann_mask: int32 [512, 1024], P('gy', 'gz'), may hold values 0 or 1
- tile_table: int32 [8, 32, 64], P(None, 'gy', 'gz'), may hold values from 0 to 127, as said below
- w_in: bfloat16 [256, 24], replicated, may hold values from -1.25 to 1.25
- b_in: float32 [256], replicated, may hold values from -3 to 3
- w_mid: bfloat16 [256, 256], replicated, may hold values from -0.375 to 0.375
- b_mid: float32 [256], replicated, may hold values from -3 to 3
- w_out: bfloat16 [6, 256], replicated, may hold values from -0.375 to 0.375
- b_out: float32 [6], replicated, may hold values from -3 to 3
Outputs:
- stepped: bfloat16 [3, 128, 512, 1024], P(None, None, 'gy', 'gz')
- prediction: float32 [6, 1048576], P(None, ('gy', 'gz'))
- loss: float32 [], replicated
- grad_w_in: float32 [256, 24], replicated
- grad_b_in: float32 [256], replicated
- grad_w_mid: float32 [256, 256], replicated
- grad_b_mid: float32 [256], replicated
- grad_w_out: float32 [6, 256], replicated
- grad_b_out: float32 [6], replicated
The draws below stay inside these ranges and needn't reach their ends.
Inputs may be any that keep to these rules, and one draw needn't show every extreme that they name: `tile_table`: within the tiles of one device's block of the table every slot number appears exactly once.
All inputs are finite; a program needn't handle non-finite values. No bound on the sum of `wall_mask` or of `hartmann_mask` on one device may be relied on, other than what follows from the above.
Results may differ from the reference program's by a relative error of at most 0.0021.
Values may be sent and summed in bfloat16 or wider, within the bound.
A program may use at most 192 MiB of HBM per device.

```python
import jax
import jax.numpy as jnp
from jax import lax

STATIONS = 128
CY = 32
CZ = 128
TILE = 16
BLOCK = 4
HID = 256
NY = 512
NZ = 1024
TILE_DEV = 128
PTS = 64
SAMPLES = 1048576
N_GY = 16
N_GZ = 8


def draw_velocity(key, part):
    key = jax.random.fold_in(key, 11)
    across = (jnp.arange(NY, dtype=jnp.float32) / NY)[:, None]
    upward = (jnp.arange(NZ, dtype=jnp.float32) / NZ)[None, :]
    base = jnp.clip(jax.random.normal(key, (3, STATIONS, NY, NZ), jnp.float32), -2.5, 2.5)
    profile = (1.0 + across) * (1.0 + 0.5 * upward)
    return base * profile


def draw_tile_table(key, part):
    key = jax.random.fold_in(key, 23)
    groups_y = NY // CY
    groups_z = NZ // CZ
    device_keys = jax.random.split(key, groups_y * groups_z)
    orders = jax.vmap(lambda sub_key: jax.random.permutation(sub_key, TILE_DEV))(device_keys)
    local_x = STATIONS // TILE
    local_y = CY // TILE
    local_z = CZ // TILE
    table = orders.reshape(groups_y, groups_z, local_x, local_y, local_z).transpose(2, 0, 3, 1, 4)
    return table.reshape(local_x, groups_y * local_y, groups_z * local_z).astype(jnp.int32)


def set_ends(array, stream_key, smallest, largest):
    dims = array.shape
    index_at = [jax.random.randint(jax.random.fold_in(stream_key, axis), (), 0, dims[axis]) for axis in range(len(dims))]
    array = array.at[tuple(index_at)].set(smallest)
    longest = dims.index(max(dims))
    index_at[longest] = (index_at[longest] + 1) % dims[longest]
    return array.at[tuple(index_at)].set(largest)


def bell_draw(key, extent, width, most, kind=jnp.bfloat16):
    return jnp.clip(width * jax.random.normal(key, extent, jnp.float32), -most, most).astype(kind)


def setup_inputs(seed: int = 0) -> dict:
    seeds = jax.random.split(jax.random.key(seed), 11)
    return {
        "velocity": draw_velocity(jax.random.fold_in(seeds[10], 71), 0),
        "wall_mask": set_ends((jax.random.randint(seeds[1], (NY, NZ), 0, 8) < 1).astype(jnp.int32), jax.random.fold_in(seeds[1], 1), 0, 1),
        "hartmann_mask": set_ends((jax.random.randint(seeds[2], (NY, NZ), 0, 4) < 1).astype(jnp.int32), jax.random.fold_in(seeds[2], 1), 0, 1),
        "tile_table": draw_tile_table(jax.random.fold_in(seeds[10], 71), 0),
        "w_in": bell_draw(seeds[4], (HID, 24), 24 ** -0.5, 1.25),
        "b_in": bell_draw(seeds[5], (HID,), 0.5, 3.0, jnp.float32),
        "w_mid": bell_draw(seeds[6], (HID, HID), HID ** -0.5, 0.375),
        "b_mid": bell_draw(seeds[7], (HID,), 0.5, 3.0, jnp.float32),
        "w_out": bell_draw(seeds[8], (6, HID), HID ** -0.5, 0.375),
        "b_out": bell_draw(seeds[9], (6,), 0.5, 3.0, jnp.float32),
    }


time_step = 0.2
viscosity = 0.5
stuart_number = 1.0
stress_pairs = ((0, 0), (1, 1), (2, 2), (0, 1), (0, 2), (1, 2))


def assemble(tile_rows):
    tile_count = tile_rows.shape[0]
    points_edge = TILE // BLOCK
    half_block = BLOCK // 2
    cell_values = tile_rows.astype(jnp.float32).reshape(tile_count, 3, points_edge, 2, half_block, points_edge, 2, half_block, points_edge, 2, half_block)
    sub_means = jnp.mean(cell_values, axis=(4, 7, 10))
    inputs = sub_means.transpose(1, 3, 5, 7, 0, 2, 4, 6).reshape(24, -1)
    point_means = jnp.mean(sub_means, axis=(3, 5, 7))
    stresses = []
    for left_comp, right_comp in stress_pairs:
        product = jnp.mean(cell_values[:, left_comp] * cell_values[:, right_comp], axis=(2, 3, 5, 6, 8, 9))
        stresses.append(product - point_means[:, left_comp] * point_means[:, right_comp])
    targets = jnp.stack(stresses).reshape(6, -1)
    return jnp.concatenate([inputs, targets], axis=0).astype(jnp.bfloat16)


def silu_slope(value):
    sigma = jax.nn.sigmoid(value)
    return sigma * (1.0 + value * (1.0 - sigma))


def reference(velocity, wall_mask, hartmann_mask, tile_table, w_in, b_in, w_mid, b_mid, w_out, b_out):
    fluid = (1 - wall_mask).astype(jnp.float32)
    factor = stuart_number * (1.0 + hartmann_mask.astype(jnp.float32))

    def plane(index):
        current = lax.dynamic_index_in_dim(velocity, index, 1, keepdims=False) * fluid
        behind = lax.dynamic_index_in_dim(velocity, jnp.mod(index - 1, STATIONS), 1, keepdims=False) * fluid
        ahead_plane = lax.dynamic_index_in_dim(velocity, jnp.mod(index + 1, STATIONS), 1, keepdims=False) * fluid
        padded = jnp.pad(current, ((0, 0), (1, 1), (1, 1)))
        north_face = padded[:, 2:, 1:-1]
        south_face = padded[:, :-2, 1:-1]
        upper_face = padded[:, 1:-1, 2:]
        lower_face = padded[:, 1:-1, :-2]
        laplace = ahead_plane + behind + north_face + south_face + upper_face + lower_face - 6.0 * current
        advect = current[0] * ((ahead_plane - behind) * 0.5) + current[1] * ((north_face - south_face) * 0.5) + current[2] * ((upper_face - lower_face) * 0.5)
        lorentz = jnp.concatenate([-factor * current[:2], jnp.zeros_like(current[2:])], axis=0)
        return ((current + time_step * (viscosity * laplace - advect + lorentz)) * fluid).astype(jnp.bfloat16)

    stepped = lax.map(plane, jnp.arange(STATIONS, dtype=jnp.int32)).transpose(1, 0, 2, 3)

    tiles_x = STATIONS // TILE
    tiles_y = NY // TILE
    tiles_z = NZ // TILE

    def slab(index):
        block_cells = lax.dynamic_slice_in_dim(stepped, index * TILE, TILE, axis=1)
        tile_rows = block_cells.reshape(3, TILE, tiles_y, TILE, tiles_z, TILE).transpose(2, 4, 0, 1, 3, 5).reshape(tiles_y * tiles_z, 3 * TILE ** 3)
        return assemble(tile_rows).reshape(30, tiles_y * tiles_z, PTS)

    slabs = lax.map(slab, jnp.arange(tiles_x, dtype=jnp.int32))
    samples = slabs.transpose(0, 2, 1, 3).reshape(tiles_x * tiles_y * tiles_z, 30, PTS)

    devices = N_GY * N_GZ
    per_peer = TILE_DEV // devices
    y_index = jnp.arange(tiles_y, dtype=jnp.int32)[None, :, None]
    z_index = jnp.arange(tiles_z, dtype=jnp.int32)[None, None, :]
    source = (y_index // (CY // TILE)) * N_GZ + z_index // (CZ // TILE)
    batch_rows = (tile_table // per_peer) * TILE_DEV + source * per_peer + tile_table % per_peer
    batch_rows = batch_rows.reshape(-1).astype(jnp.int32)
    ordered = jnp.zeros_like(samples).at[batch_rows].set(samples)
    batches = ordered.transpose(1, 0, 2).reshape(30, devices, TILE_DEV * PTS).transpose(1, 0, 2)

    scale = 2.0 / (6 * SAMPLES)
    weight_in = w_in.astype(jnp.float32)
    weight_mid = w_mid.astype(jnp.float32)
    weight_out = w_out.astype(jnp.float32)

    def train(carry, packed):
        inputs = packed[:24].astype(jnp.float32)
        targets = packed[24:].astype(jnp.float32)
        first_pre = jnp.dot(weight_in, inputs) + b_in[:, None]
        first_act = jax.nn.silu(first_pre).astype(jnp.bfloat16).astype(jnp.float32)
        second_pre = jnp.dot(weight_mid, first_act) + b_mid[:, None]
        second_act = jax.nn.silu(second_pre).astype(jnp.bfloat16).astype(jnp.float32)
        prediction = jnp.dot(weight_out, second_act) + b_out[:, None]
        residual = prediction - targets
        squares = jnp.sum(residual * residual)
        pred_grad = (residual * scale).astype(jnp.bfloat16).astype(jnp.float32)
        grad_w_out = jnp.dot(pred_grad, second_act.T)
        grad_b_out = jnp.sum(pred_grad, axis=1)
        second_grad = (jnp.dot(weight_out.T, pred_grad) * silu_slope(second_pre)).astype(jnp.bfloat16).astype(jnp.float32)
        grad_w_mid = jnp.dot(second_grad, first_act.T)
        grad_b_mid = jnp.sum(second_grad, axis=1)
        first_grad = (jnp.dot(weight_mid.T, second_grad) * silu_slope(first_pre)).astype(jnp.bfloat16).astype(jnp.float32)
        grad_w_in = jnp.dot(first_grad, inputs.T)
        grad_b_in = jnp.sum(first_grad, axis=1)
        terms = (grad_w_in, grad_b_in, grad_w_mid, grad_b_mid, grad_w_out, grad_b_out, squares)
        carry = tuple(total + term for total, term in zip(carry, terms))
        return carry, prediction

    start = (jnp.zeros((HID, 24), jnp.float32), jnp.zeros((HID,), jnp.float32), jnp.zeros((HID, HID), jnp.float32), jnp.zeros((HID,), jnp.float32), jnp.zeros((6, HID), jnp.float32), jnp.zeros((6,), jnp.float32), jnp.zeros((), jnp.float32))
    totals, predictions = lax.scan(train, start, batches)
    prediction = predictions.transpose(1, 0, 2).reshape(6, SAMPLES)
    loss = totals[6] / (6 * SAMPLES)
    return stepped, prediction, loss, totals[0], totals[1], totals[2], totals[3], totals[4], totals[5]
```

```python
import functools

import jax
import jax.numpy as jnp
from jax import lax
from jax.experimental import pallas as pl
from jax.experimental.pallas import tpu as pltpu
from jax.sharding import PartitionSpec as P

MESH = pl.DeviceIdType.MESH
STATIONS = 128
CY = 32
CZ = 128
HID = 256
N_GY = 16
N_GZ = 8
TILES = 128
SAMPLES = 1048576
ROWS = 3 * STATIONS * CY
SLABS = 8
LANES = 1024
PART = 512
F32 = jnp.float32
BF16 = jnp.bfloat16
PAIRS = ((0, 0), (1, 1), (2, 2), (0, 1), (0, 2), (1, 2))
NT = (((1,), (1,)), ((), ()))


def iota(shape, dim):
    return lax.broadcasted_iota(jnp.int32, shape, dim)


def wait_bytes(ref, sem):
    pltpu.make_async_copy(ref, ref, sem).wait()


def pack_edges(v, fluid, edge_lo, edge_hi, columns):
    for c in range(3):
        first = c * STATIONS * CY
        edge_lo[pl.ds(c * STATIONS, STATIONS), :] = v[pl.ds(first, STATIONS, stride=CY), :] * fluid[0:1, :]
        edge_hi[pl.ds(c * STATIONS, STATIONS), :] = (
            v[pl.ds(first + CY - 1, STATIONS, stride=CY), :] * fluid[CY - 1 : CY, :]
        )
    pair = iota((8, 128), 1) // 2

    def station(s, acc):
        here = pair == s
        out = []
        for c in range(3):
            for h in range(2):
                for j in range(4):
                    cells = v[pl.ds((c * STATIONS + h * 64 + s) * CY + 8 * j, 8), :]
                    moved = pltpu.roll(cells, 2 * s + 1, 1)
                    out.append(jnp.where(here, moved, acc[len(out)]))
        return tuple(out)

    packed = lax.fori_loop(0, 64, station, tuple(jnp.zeros((8, 128), F32) for _ in range(24)))
    odd = iota((8, 128), 1) % 2 == 1
    for c in range(3):
        for h in range(2):
            for j in range(4):
                mask = fluid[8 * j : 8 * j + 8, :]
                ends = jnp.where(odd, mask[:, 0:1], mask[:, CZ - 1 : CZ])
                columns[pl.ds((c * 2 + h) * CY + 8 * j, 8), :] = packed[(c * 2 + h) * 4 + j] * ends


def halo_kernel(vel, wall, lo_out, hi_out, col_out, v, fluid, edge_lo, edge_hi, columns, got_lo, got_hi, got_left, got_right, load, send, recv):
    y = lax.axis_index("gy")
    z = lax.axis_index("gz")
    below = ((y + N_GY - 1) % N_GY, z)
    above = ((y + 1) % N_GY, z)
    left = (y, (z + N_GZ - 1) % N_GZ)
    right = (y, (z + 1) % N_GZ)
    fetch = pltpu.make_async_copy(vel, v, load)
    fetch.start()
    barrier = pltpu.get_barrier_semaphore()
    for peer in (below, above, left, right):
        pl.semaphore_signal(barrier, inc=1, device_id=peer, device_id_type=MESH)
    fluid[...] = (1 - wall[...]).astype(F32)
    fetch.wait()
    pack_edges(v, fluid, edge_lo, edge_hi, columns)
    pl.semaphore_wait(barrier, 4)
    copies = []
    for k, (src, dst, peer) in enumerate(
        ((edge_lo, got_hi, below), (edge_hi, got_lo, above), (columns, got_right, left), (columns, got_left, right))
    ):
        copy = pltpu.make_async_remote_copy(
            src, dst, send.at[k], recv.at[k], device_id=peer, device_id_type=MESH
        )
        copy.start()
        copies.append(copy)
    for copy in copies:
        copy.wait()
    lo_out[...] = got_lo[...] * jnp.where(y > 0, 1.0, 0.0)
    hi_out[...] = got_hi[...] * jnp.where(y < N_GY - 1, 1.0, 0.0)
    has_left = jnp.where(z > 0, 1.0, 0.0)
    has_right = jnp.where(z < N_GZ - 1, 1.0, 0.0)
    odd = iota((8, 128), 1) % 2 == 1
    for k in range(24):
        rows = pl.ds(8 * k, 8)
        col_out[rows, :] = jnp.where(odd, got_right[rows, :] * has_right, pltpu.roll(got_left[rows, :] * has_left, 2, 1))


def halo_call(vel, wall):
    return pl.pallas_call(
        halo_kernel,
        name="halo",
        out_shape=[
            jax.ShapeDtypeStruct((384, 128), F32),
            jax.ShapeDtypeStruct((384, 128), F32),
            jax.ShapeDtypeStruct((192, 128), F32),
        ],
        in_specs=[pl.BlockSpec(memory_space=pl.ANY), pl.BlockSpec(memory_space=pltpu.VMEM)],
        out_specs=[pl.BlockSpec(memory_space=pltpu.VMEM)] * 3,
        scratch_shapes=[
            pltpu.VMEM((ROWS, 128), F32),
            pltpu.VMEM((CY, 128), F32),
            pltpu.VMEM((384, 128), F32),
            pltpu.VMEM((384, 128), F32),
            pltpu.VMEM((192, 128), F32),
            pltpu.VMEM((384, 128), F32),
            pltpu.VMEM((384, 128), F32),
            pltpu.VMEM((192, 128), F32),
            pltpu.VMEM((192, 128), F32),
            pltpu.SemaphoreType.DMA,
            pltpu.SemaphoreType.DMA((4,)),
            pltpu.SemaphoreType.DMA((4,)),
        ],
        compiler_params=pltpu.CompilerParams(collective_id=0, has_side_effects=True, vmem_limit_bytes=24 << 20),
    )(vel, wall)


def stencil_station(v, lo, hi, col, tables, stepped, rounded, st, s):
    ahead = lax.rem(st + 1, STATIONS)
    behind = lax.rem(st + STATIONS - 1, STATIONS)
    half = st // 64
    shift = 126 - 2 * lax.rem(st, 64)
    first_row = iota((8, 128), 0) == 0
    last_row = iota((8, 128), 0) == 7
    first_lane = iota((8, 128), 1) == 0
    last_lane = iota((8, 128), 1) == CZ - 1

    def cells(c, t, j):
        return v[pl.ds((c * STATIONS + t) * CY + 8 * j, 8), :]

    m = [[cells(c, st, j) * tables[pl.ds(8 * j, 8), :] for j in range(4)] for c in range(3)]
    minus = [[1.0 - m[c][j] for j in range(4)] for c in range(3)]
    plus = [[1.0 + m[c][j] for j in range(4)] for c in range(3)]
    for c in range(3):
        edge_lo = jnp.broadcast_to(lo[pl.ds(c * STATIONS + st, 1), :], (8, 128))
        edge_hi = jnp.broadcast_to(hi[pl.ds(c * STATIONS + st, 1), :], (8, 128))
        down = [edge_lo] + [pltpu.roll(m[c][j], 1, 0) for j in range(4)]
        up = [pltpu.roll(m[c][j], 7, 0) for j in range(4)] + [edge_hi]
        results = []
        for j in range(4):
            south = jnp.where(first_row, down[j], down[j + 1])
            north = jnp.where(last_row, up[j + 1], up[j])
            ends = pltpu.roll(col[pl.ds((c * 2 + half) * CY + 8 * j, 8), :], shift, 1)
            lower = jnp.where(first_lane, ends, pltpu.roll(m[c][j], 1, 1))
            upper = jnp.where(last_lane, ends, pltpu.roll(m[c][j], CZ - 1, 1))
            total = minus[0][j] * cells(c, ahead, j) + plus[0][j] * cells(c, behind, j)
            total = total + (minus[1][j] * north + plus[1][j] * south)
            total = total + (minus[2][j] * upper + plus[2][j] * lower)
            own = tables[pl.ds(64 + 8 * j, 8), :] if c < 2 else 4.0
            total = total + own * m[c][j]
            results.append(total * tables[pl.ds(32 + 8 * j, 8), :])
        for k in range(2):
            value = jnp.concatenate(results[2 * k : 2 * k + 2], axis=0).astype(BF16)
            stepped[pl.ds(pl.multiple_of((c * STATIONS + st) * CY + 16 * k, 16), 16), :] = value
            rounded[pl.ds((c * 16 + s) * CY + 16 * k, 16), :] = value.astype(F32)


def pool_slab(rounded, feat):
    residue = iota((8, 128), 1) % 4
    merged = [None] * 30

    def put(f, r, value, source):
        shift = (r - source) % 128
        value = pltpu.roll(value, shift, 1) if shift else value
        merged[f] = value if merged[f] is None else jnp.where(residue == r, value, merged[f])

    for r in range(4):
        sums = [[None] * 4 for _ in range(3)]
        products = [None] * 6
        for dx in range(4):
            for dy in range(4):
                q = (dx // 2) * 2 + dy // 2
                u = [rounded[pl.ds((c * 16 + 4 * r + dx) * CY + dy, 8, stride=4), :] for c in range(3)]
                for c in range(3):
                    sums[c][q] = u[c] if sums[c][q] is None else sums[c][q] + u[c]
                for k, (a, b) in enumerate(PAIRS):
                    value = u[a] * u[b]
                    products[k] = value if products[k] is None else products[k] + value
        means = []
        for c in range(3):
            point = None
            for q in range(4):
                two = sums[c][q] + pltpu.roll(sums[c][q], 127, 1)
                put(c * 8 + 2 * q, r, two, 0)
                put(c * 8 + 2 * q + 1, r, two, 2)
                point = two if point is None else point + two
            means.append((point + pltpu.roll(point, 126, 1)) * (1.0 / 64))
        for k, (a, b) in enumerate(PAIRS):
            two = products[k] + pltpu.roll(products[k], 127, 1)
            four = two + pltpu.roll(two, 126, 1)
            put(24 + k, r, four * (1.0 / 64) - means[a] * means[b], 0)
    for f in range(24):
        feat[pl.ds(8 * f, 8), :] = merged[f] * 0.125
    for f in range(24, 30):
        feat[pl.ds(8 * f, 8), :] = merged[f].astype(BF16).astype(F32)


def column_table(row):
    wide = jnp.broadcast_to(row, (128, HID))
    return jnp.concatenate([jnp.transpose(wide[:, :128]), jnp.transpose(wide[:, 128:])], axis=0)


def prepare_weights(w_in, b_in, w_mid, b_mid, w_out, b_out, win, wmid, wmid_t, wout, wout_t, bias_mid, bias_out, tmp):
    lane = iota((HID, 128), 1)
    bias = column_table(b_in[...]) * 0.5
    high = bias.astype(BF16).astype(F32)
    tmp[...] = jnp.zeros_like(tmp)
    tmp[:, 0:24] = w_in[...].astype(F32) * 0.5
    full = tmp[...]
    full = jnp.where(lane == 30, high, jnp.where(lane == 31, bias - high, full))
    win[...] = full[:, 0:32].astype(BF16)
    mid = w_mid[...].astype(F32) * 0.5
    wmid[...] = mid.astype(BF16)
    wmid_t[...] = jnp.transpose(mid).astype(BF16)
    bias_mid[...] = column_table(b_mid[...]) * 0.5
    for h in range(2):
        tmp[pl.ds(0, 128), :] = jnp.zeros((128, 128), F32)
        tmp[pl.ds(0, 6), :] = w_out[:, 128 * h : 128 * h + 128].astype(F32)
        wout[:, 128 * h : 128 * h + 128] = tmp[pl.ds(0, 16), :].astype(BF16)
        wout_t[pl.ds(128 * h, 128), :] = (jnp.transpose(tmp[pl.ds(0, 128), :])[:, 0:16] * 0.5).astype(BF16)
    row = iota((8, 128), 0)
    table = jnp.where(row >= 6, 1.0, 0.0)
    for k in range(6):
        table = jnp.where(row == k, b_out[k], table)
    bias_out[...] = table


def widen(table, lanes):
    return jnp.concatenate([table] * (lanes // 128), axis=1)


def lane_sum(value):
    total = value[:, 0:128]
    for k in range(1, value.shape[1] // 128):
        total = total + value[:, 128 * k : 128 * k + 128]
    return total


def train_part(x, targets, win, wmid, wmid_t, wout, wout_t, bias_mid, bias_out, pred, g_in, g_mid, g_out, g_bmid, g_bout, g_loss):
    n = x.shape[1]
    h1 = jnp.dot(win[...], x, preferred_element_type=F32)
    t1 = jnp.tanh(h1)
    p1 = 1.0 + t1
    a1 = h1 * p1
    slope1 = p1 + a1 * (2.0 - p1)
    act1 = a1.astype(BF16)
    h2 = jnp.dot(wmid[...], act1, preferred_element_type=F32) + widen(bias_mid[...], n)
    p2 = 1.0 + jnp.tanh(h2)
    a2 = h2 * p2
    slope2 = p2 + a2 * (2.0 - p2)
    act2 = a2.astype(BF16)
    prediction = jnp.dot(wout[...], act2, preferred_element_type=F32)[0:8] + widen(bias_out[...], n)
    pred[...] = prediction
    residual = prediction - targets
    g_loss[...] += lane_sum(residual * residual)
    grad = (residual * (2.0 / (6 * SAMPLES))).astype(BF16).astype(F32)
    g_bout[...] += lane_sum(grad)
    grad = jnp.concatenate([grad, jnp.zeros_like(grad)], axis=0).astype(BF16)
    g_out[...] += lax.dot_general(grad, act2, NT, preferred_element_type=F32)
    d2 = jnp.dot(wout_t[...], grad, preferred_element_type=F32) * slope2
    g_bmid[...] += lane_sum(d2)
    grad2 = d2.astype(BF16)
    g_mid[...] += lax.dot_general(grad2, act1, NT, preferred_element_type=F32)
    d1 = jnp.dot(wmid_t[...], grad2, preferred_element_type=F32) * slope1
    grad1 = d1.astype(BF16)
    g_in[...] += lax.dot_general(x, grad1, NT, preferred_element_type=F32)


def scatter_slab(a, pred, table, ordered):
    lane = iota((8, 128), 1)
    point = lane % 64
    quarter = point // 4 % 4
    source = 4 * (point % 4) + point // 16
    low = lane < 64
    for b in range(2):
        blocks = [pred[:, 128 * (4 * b + q) : 128 * (4 * b + q) + 128] for q in range(4)]
        for c in range(8):
            index = source + 16 * c
            value = jnp.take_along_axis(blocks[0], index, axis=1)
            for q in range(1, 4):
                value = jnp.where(quarter == q, jnp.take_along_axis(blocks[q], index, axis=1), value)
            value = jnp.where(low, value, pltpu.roll(value, 5, 0))
            ordered[table[a * 16 + b * 8 + c]] = value[0:3]


def main_kernel(
    vel, wall, hart, table, lo, hi, col, w_in, b_in, w_mid, b_mid, w_out, b_out,
    stepped_out, grads, ordered,
    v, stepped, rounded, tables, feat, xs, targets, pred, win, wmid, wmid_t, wout, wout_t, bias_mid, bias_out, tmp,
    g_in, g_mid, g_out, g_bmid, g_bout, g_loss, load, store,
):
    def fetch(c, i):
        rows = pl.ds(c * STATIONS * CY + i * 16 * CY, 16 * CY)
        return pltpu.make_async_copy(vel.at[rows], v.at[rows], load.at[i])

    def fetches(i, act):
        for c in range(3):
            getattr(fetch(c, i), act)()

    def store_copy(c, a):
        rows = pl.ds(pl.multiple_of(c * STATIONS * CY + a * 16 * CY, 16), 16 * CY)
        return pltpu.make_async_copy(stepped.at[rows], stepped_out.at[rows], store.at[c])

    for i in (7, 0, 1, 2, 3, 4, 5, 6):
        fetches(i, "start")
    fluid = (1 - wall[...]).astype(F32)
    tables[pl.ds(0, 32), :] = fluid
    tables[pl.ds(32, 32), :] = fluid * 0.1
    tables[pl.ds(64, 32), :] = 2.0 - 2.0 * hart[...].astype(F32)
    prepare_weights(w_in, b_in, w_mid, b_mid, w_out, b_out, win, wmid, wmid_t, wout, wout_t, bias_mid, bias_out, tmp)
    for ref in (g_in, g_mid, g_out, g_bmid, g_bout, g_loss):
        ref[...] = jnp.zeros_like(ref)
    feat[pl.ds(240, 16), :] = jnp.ones((16, 128), F32)
    for i in (7, 0, 1, 2, 3, 4, 5, 6):
        fetches(i, "wait")

    def slab(a, carry):
        def station(s, inner):
            stencil_station(v, lo, hi, col, tables, stepped, rounded, a * 16 + s, s)
            return inner

        lax.fori_loop(0, 16, station, 0)
        for c in range(3):
            store_copy(c, a).start()
        pool_slab(rounded, feat)
        for yp in range(8):
            lanes = slice(128 * yp, 128 * yp + 128)
            xs[:, lanes] = feat[pl.ds(yp, 32, stride=8), :].astype(BF16)
            targets[:, lanes] = feat[pl.ds(192 + yp, 8, stride=8), :]
        for k in range(LANES // PART):
            lanes = slice(PART * k, PART * k + PART)
            train_part(
                xs[:, lanes], targets[:, lanes], win, wmid, wmid_t, wout, wout_t, bias_mid, bias_out,
                pred.at[:, lanes], g_in, g_mid, g_out, g_bmid, g_bout, g_loss,
            )
        scatter_slab(a, pred, table, ordered)
        return carry

    lax.fori_loop(0, SLABS, slab, 0)
    for c in range(3):
        wait_bytes(stepped.at[pl.ds(0, STATIONS * CY)], store.at[c])
    for t in range(64):
        grads[t // 5, t % 5] = g_mid[pl.ds(8 * (t // 2), 8), 128 * (t % 2) : 128 * (t % 2) + 128]
    for k in range(8):
        t = 64 + k
        grads[t // 5, t % 5] = g_in[pl.ds(8 * (k // 2), 8), 128 * (k % 2) : 128 * (k % 2) + 128]
    row = iota((8, 128), 0)
    lane = iota((8, 128), 1)
    sums_out = jnp.sum(g_bout[...], axis=1, keepdims=True)
    last = jnp.sum(jnp.where((lane == row + 8) & (row < 6), sums_out, 0.0), axis=0, keepdims=True)
    loss = jnp.sum(jnp.sum(g_loss[...], axis=1, keepdims=True), axis=0, keepdims=True)
    last = jnp.where(lane[0:1] == 0, loss, last)
    for k in range(2):
        t = 72 + k
        bias = jnp.sum(jnp.transpose(g_bmid[pl.ds(128 * k, 128), :]), axis=0, keepdims=True)
        value = g_out[pl.ds(0, 8), 128 * k : 128 * k + 128]
        grads[t // 5, t % 5] = jnp.where(row == 6, bias, jnp.where(row == 7, last, value))
    for t in range(74, 80):
        grads[t // 5, t % 5] = jnp.zeros((8, 128), F32)


def main_call(vel, wall, hart, table, lo, hi, col, w_in, b_in, w_mid, b_mid, w_out, b_out):
    vm = pl.BlockSpec(memory_space=pltpu.VMEM)
    sm = pl.BlockSpec(memory_space=pltpu.SMEM)
    anywhere = pl.BlockSpec(memory_space=pl.ANY)
    return pl.pallas_call(
        main_kernel,
        name="step_train",
        out_shape=[
            jax.ShapeDtypeStruct((ROWS, 128), BF16),
            jax.ShapeDtypeStruct((16, 5, 8, 128), F32),
            jax.ShapeDtypeStruct((TILES, 3, 128), F32),
        ],
        in_specs=[anywhere, vm, vm, sm, vm, vm, vm, vm, vm, vm, vm, vm, sm],
        out_specs=[anywhere, vm, vm],
        scratch_shapes=[
            pltpu.VMEM((ROWS, 128), F32),
            pltpu.VMEM((ROWS, 128), BF16),
            pltpu.VMEM((3 * 16 * CY, 128), F32),
            pltpu.VMEM((96, 128), F32),
            pltpu.VMEM((256, 128), F32),
            pltpu.VMEM((32, LANES), BF16),
            pltpu.VMEM((8, LANES), F32),
            pltpu.VMEM((8, LANES), F32),
            pltpu.VMEM((HID, 32), BF16),
            pltpu.VMEM((HID, HID), BF16),
            pltpu.VMEM((HID, HID), BF16),
            pltpu.VMEM((16, HID), BF16),
            pltpu.VMEM((HID, 16), BF16),
            pltpu.VMEM((HID, 128), F32),
            pltpu.VMEM((8, 128), F32),
            pltpu.VMEM((HID, 128), F32),
            pltpu.VMEM((32, HID), F32),
            pltpu.VMEM((HID, HID), F32),
            pltpu.VMEM((16, HID), F32),
            pltpu.VMEM((HID, 128), F32),
            pltpu.VMEM((8, 128), F32),
            pltpu.VMEM((8, 128), F32),
            pltpu.SemaphoreType.DMA((8,)),
            pltpu.SemaphoreType.DMA((3,)),
        ],
        compiler_params=pltpu.CompilerParams(vmem_limit_bytes=48 << 20),
    )(vel, wall, hart, table, lo, hi, col, w_in, b_in, w_mid, b_mid, w_out, b_out)


def share_kernel(
    g, p, pred_out, loss_out, in_out, bin_out, mid_out, bmid_out, out_out, bout_out,
    part, mine, column, total, hop, got, s0, r0, s1, r1, s2, r2, s3, r3, s4, r4,
):
    y = lax.axis_index("gy")
    z = lax.axis_index("gz")
    barrier = pltpu.get_barrier_semaphore()
    for d in range(1, N_GY):
        pl.semaphore_signal(barrier, inc=1, device_id=((y + d) % N_GY, z), device_id_type=MESH)
    for d in range(1, N_GZ):
        pl.semaphore_signal(barrier, inc=1, device_id=(y, (z + d) % N_GZ), device_id_type=MESH)
    pl.semaphore_wait(barrier, N_GY + N_GZ - 2)

    def send(src, dst, ss, rs, qy, qz):
        pltpu.make_async_remote_copy(src, dst, ss, rs, device_id=(qy, qz), device_id_type=MESH).start()

    for d in range(1, N_GY):
        q = (y + d) % N_GY
        send(g.at[q], part.at[y], s0, r0, q, z)
    for d in range(1, N_GZ):
        q = (z + d) % N_GZ
        send(p.at[:, q], hop.at[z], s1, r1, y, q)
    hop[z] = p[:, z]
    part[y] = g[y]
    wait_bytes(part.at[pl.ds(0, N_GY - 1)], r0)
    column[z] = jnp.sum(part[...], axis=0)
    for d in range(1, N_GZ):
        q = (z + d) % N_GZ
        send(column.at[z], column.at[z], s2, r2, y, q)
    wait_bytes(hop.at[pl.ds(0, N_GZ - 1)], r1)
    for d in range(1, N_GY):
        q = (y + d) % N_GY
        send(hop.at[:, q], got.at[y], s3, r3, q, z)
    got[y] = hop[:, y]
    wait_bytes(column.at[pl.ds(0, N_GZ - 1)], r2)
    mine[...] = jnp.sum(column[...], axis=0)
    for d in range(1, N_GY):
        q = (y + d) % N_GY
        send(mine, total.at[y], s4, r4, q, z)
    total[y] = mine[...]
    wait_bytes(got.at[pl.ds(0, N_GY - 1)], r3)
    low = iota((3, 128), 1) < 64
    for j in range(TILES // 2):
        first = got[(2 * j) // N_GZ, (2 * j) % N_GZ]
        second = got[(2 * j + 1) // N_GZ, (2 * j + 1) % N_GZ]
        lanes = slice(128 * j, 128 * j + 128)
        pred_out[0:3, lanes] = jnp.where(low, first, pltpu.roll(second, 64, 1))
        pred_out[3:6, lanes] = jnp.where(low, pltpu.roll(first, 64, 1), second)
    wait_bytes(total.at[pl.ds(0, N_GY - 1)], r4)
    for t in range(64):
        mid_out[pl.ds(8 * (t // 2), 8), 128 * (t % 2) : 128 * (t % 2) + 128] = total[t // 5, t % 5]
    for h in range(2):
        rows = jnp.concatenate([total[(64 + 2 * k + h) // 5, (64 + 2 * k + h) % 5] for k in range(4)], axis=0)
        padded = jnp.concatenate([rows, jnp.zeros((96, 128), F32)], axis=0)
        in_out[pl.ds(128 * h, 128), :] = jnp.transpose(padded)[:, 0:24]
        bin_out[:, 128 * h : 128 * h + 128] = rows[30:31]
        last = total[(72 + h) // 5, (72 + h) % 5]
        out_out[:, 128 * h : 128 * h + 128] = last[0:6]
        bmid_out[:, 128 * h : 128 * h + 128] = last[6:7]
        if h == 0:
            loss_out[...] = last[7:8] * (1.0 / (6 * SAMPLES))
            bout_out[...] = last[7:8]
    wait_bytes(part.at[pl.ds(0, N_GY - 1)], s0)
    wait_bytes(hop.at[pl.ds(0, N_GZ - 1)], s1)
    wait_bytes(column.at[pl.ds(0, N_GZ - 1)], s2)
    wait_bytes(got.at[pl.ds(0, N_GY - 1)], s3)
    wait_bytes(total.at[pl.ds(0, N_GY - 1)], s4)


def share_call(grads, ordered):
    vm = pl.BlockSpec(memory_space=pltpu.VMEM)
    return pl.pallas_call(
        share_kernel,
        name="share",
        out_shape=[
            jax.ShapeDtypeStruct((6, 64 * 128), F32),
            jax.ShapeDtypeStruct((1, 128), F32),
            jax.ShapeDtypeStruct((HID, 24), F32),
            jax.ShapeDtypeStruct((1, HID), F32),
            jax.ShapeDtypeStruct((HID, HID), F32),
            jax.ShapeDtypeStruct((1, HID), F32),
            jax.ShapeDtypeStruct((6, HID), F32),
            jax.ShapeDtypeStruct((1, 128), F32),
        ],
        in_specs=[vm, vm],
        out_specs=[vm] * 8,
        scratch_shapes=[
            pltpu.VMEM((N_GY, 5, 8, 128), F32),
            pltpu.VMEM((5, 8, 128), F32),
            pltpu.VMEM((N_GZ, 5, 8, 128), F32),
            pltpu.VMEM((N_GY, 5, 8, 128), F32),
            pltpu.VMEM((N_GZ, N_GY, 3, 128), F32),
            pltpu.VMEM((N_GY, N_GZ, 3, 128), F32),
        ]
        + [pltpu.SemaphoreType.DMA] * 10,
        compiler_params=pltpu.CompilerParams(collective_id=1, has_side_effects=True, vmem_limit_bytes=24 << 20),
    )(grads, ordered)


def on_device(velocity, wall_mask, hartmann_mask, tile_table, w_in, b_in, w_mid, b_mid, w_out, b_out):
    vel = velocity.reshape(ROWS, CZ)
    lo, hi, col = halo_call(vel, wall_mask)
    stepped, grads, ordered = main_call(
        vel, wall_mask, hartmann_mask, tile_table.reshape(TILES), lo, hi, col,
        w_in, b_in.reshape(1, HID), w_mid, b_mid.reshape(1, HID), w_out, b_out,
    )
    prediction, loss, grad_in, grad_bin, grad_mid, grad_bmid, grad_out, last = share_call(
        grads, ordered.reshape(N_GY, N_GZ, 3, 128)
    )
    return (
        stepped.reshape(3, STATIONS, CY, CZ),
        prediction,
        loss[0, 0],
        grad_in,
        grad_bin.reshape(HID),
        grad_mid,
        grad_bmid.reshape(HID),
        grad_out,
        last[0, 8:14],
    )


def solution(mesh):
    whole = P()
    in_specs = (P(None, None, "gy", "gz"), P("gy", "gz"), P("gy", "gz"), P(None, "gy", "gz")) + (whole,) * 6
    out_specs = (P(None, None, "gy", "gz"), P(None, ("gy", "gz"))) + (whole,) * 7
    return jax.shard_map(on_device, mesh=mesh, in_specs=in_specs, out_specs=out_specs, check_vma=False)
```

```python
import functools

import jax
import jax.numpy as jnp
from jax import lax
from jax.experimental import pallas as pl
from jax.experimental.pallas import tpu as pltpu
from jax.sharding import PartitionSpec as P

MESH = pl.DeviceIdType.MESH
STATIONS = 128
CY = 32
CZ = 128
HID = 256
N_GY = 16
N_GZ = 8
TILES = 128
SAMPLES = 1048576
ROWS = 3 * STATIONS * CY
SLABS = 8
LANES = 1024
F32 = jnp.float32
BF16 = jnp.bfloat16
PAIRS = ((0, 0), (1, 1), (2, 2), (0, 1), (0, 2), (1, 2))
NT = (((1,), (1,)), ((), ()))


def iota(shape, dim):
    return lax.broadcasted_iota(jnp.int32, shape, dim)


def wait_bytes(ref, sem):
    pltpu.make_async_copy(ref, ref, sem).wait()


def pack_edges(v, fluid, edge_lo, edge_hi):
    for c in range(3):
        first = c * STATIONS * CY
        rows = pl.ds(c * STATIONS, STATIONS)
        edge_lo[rows, :] = (v[pl.ds(first, STATIONS, stride=CY), :] * fluid[0:1, :]).astype(BF16)
        edge_hi[rows, :] = (v[pl.ds(first + CY - 1, STATIONS, stride=CY), :] * fluid[CY - 1 : CY, :]).astype(BF16)


def pack_columns(v, fluid, to_left, to_right):
    pair = iota((8, 128), 1) // 2
    odd = iota((8, 128), 1) % 2 == 1
    for c in range(3):

        def station(s, acc):
            here = pair == s
            out = []
            for h in range(2):
                for j in range(4):
                    cells = v[pl.ds((c * STATIONS + h * 64 + s) * CY + 8 * j, 8), :]
                    out.append(jnp.where(here, pltpu.roll(cells, 2 * s + 1, 1), acc[len(out)]))
            return tuple(out)

        packed = lax.fori_loop(0, 64, station, tuple(jnp.zeros((8, 128), F32) for _ in range(8)), unroll=8)
        for k in range(2):
            left, right = [], []
            for j in (2 * k, 2 * k + 1):
                mask = fluid[8 * j : 8 * j + 8, :]
                near, far = packed[j], packed[4 + j]
                right.append(jnp.where(odd, pltpu.roll(far, 1, 1), near) * mask[:, CZ - 1 : CZ])
                left.append(jnp.where(odd, far, pltpu.roll(near, 127, 1)) * mask[:, 0:1])
            rows = pl.ds(c * CY + 16 * k, 16)
            to_right[rows, :] = jnp.concatenate(right, axis=0).astype(BF16)
            to_left[rows, :] = jnp.concatenate(left, axis=0).astype(BF16)


def halo_kernel(v, wall, lo_out, hi_out, col_out, fluid, edge_lo, edge_hi, to_left, to_right, got_lo, got_hi, got_left, got_right, send, recv):
    y = lax.axis_index("gy")
    z = lax.axis_index("gz")
    below = ((y + N_GY - 1) % N_GY, z)
    above = ((y + 1) % N_GY, z)
    left = (y, (z + N_GZ - 1) % N_GZ)
    right = (y, (z + 1) % N_GZ)
    barrier = pltpu.get_barrier_semaphore()
    for peer in (below, above, left, right):
        pl.semaphore_signal(barrier, inc=1, device_id=peer, device_id_type=MESH)
    fluid[...] = (1 - wall[...]).astype(F32)
    pack_columns(v, fluid, to_left, to_right)
    pack_edges(v, fluid, edge_lo, edge_hi)
    pl.semaphore_wait(barrier, 4)
    copies = []
    for k, (src, dst, peer) in enumerate(
        ((to_left, got_right, left), (to_right, got_left, right), (edge_lo, got_hi, below), (edge_hi, got_lo, above))
    ):
        copy = pltpu.make_async_remote_copy(
            src, dst, send.at[k], recv.at[k], device_id=peer, device_id_type=MESH
        )
        copy.start()
        copies.append(copy)
    for copy in copies:
        copy.wait_recv()
    lo_out[...] = got_lo[...].astype(F32) * jnp.where(y > 0, 1.0, 0.0)
    hi_out[...] = got_hi[...].astype(F32) * jnp.where(y < N_GY - 1, 1.0, 0.0)
    has_left = jnp.where(z > 0, 1.0, 0.0)
    has_right = jnp.where(z < N_GZ - 1, 1.0, 0.0)
    odd = iota((16, 128), 1) % 2 == 1
    for c in range(3):
        for k in range(2):
            rows = pl.ds(c * CY + 16 * k, 16)
            lower = got_left[rows, :].astype(F32) * has_left
            upper = got_right[rows, :].astype(F32) * has_right
            near = jnp.where(odd, pltpu.roll(upper, 1, 1), pltpu.roll(lower, 2, 1))
            far = jnp.where(odd, upper, pltpu.roll(lower, 1, 1))
            col_out[pl.ds((c * 2) * CY + 16 * k, 16), :] = near
            col_out[pl.ds((c * 2 + 1) * CY + 16 * k, 16), :] = far
    for copy in copies:
        copy.wait_send()


def halo_call(vel, wall):
    vm = pl.BlockSpec(memory_space=pltpu.VMEM)
    return pl.pallas_call(
        halo_kernel,
        name="halo",
        out_shape=[
            jax.ShapeDtypeStruct((384, 128), F32),
            jax.ShapeDtypeStruct((384, 128), F32),
            jax.ShapeDtypeStruct((192, 128), F32),
        ],
        in_specs=[vm, vm],
        out_specs=[vm] * 3,
        scratch_shapes=[
            pltpu.VMEM((CY, 128), F32),
            pltpu.VMEM((384, 128), BF16),
            pltpu.VMEM((384, 128), BF16),
            pltpu.VMEM((96, 128), BF16),
            pltpu.VMEM((96, 128), BF16),
            pltpu.VMEM((384, 128), BF16),
            pltpu.VMEM((384, 128), BF16),
            pltpu.VMEM((96, 128), BF16),
            pltpu.VMEM((96, 128), BF16),
            pltpu.SemaphoreType.DMA((4,)),
            pltpu.SemaphoreType.DMA((4,)),
        ],
        compiler_params=pltpu.CompilerParams(collective_id=0, has_side_effects=True, vmem_limit_bytes=16 << 20),
    )(vel, wall)


def stencil_station(v, lo, hi, col, tables, stepped, rounded, st, s):
    ahead = lax.rem(st + 1, STATIONS)
    behind = lax.rem(st + STATIONS - 1, STATIONS)
    half = st // 64
    shift = 126 - 2 * lax.rem(st, 64)
    first_row = iota((8, 128), 0) == 0
    last_row = iota((8, 128), 0) == 7
    first_lane = iota((8, 128), 1) == 0
    last_lane = iota((8, 128), 1) == CZ - 1

    def cells(c, t, j):
        return v[pl.ds((c * STATIONS + t) * CY + 8 * j, 8), :]

    m = [[cells(c, st, j) * tables[pl.ds(8 * j, 8), :] for j in range(4)] for c in range(3)]
    minus = [[1.0 - m[c][j] for j in range(4)] for c in range(3)]
    plus = [[1.0 + m[c][j] for j in range(4)] for c in range(3)]
    for c in range(3):
        edge_lo = jnp.broadcast_to(lo[pl.ds(c * STATIONS + st, 1), :], (8, 128))
        edge_hi = jnp.broadcast_to(hi[pl.ds(c * STATIONS + st, 1), :], (8, 128))
        down = [edge_lo] + [pltpu.roll(m[c][j], 1, 0) for j in range(4)]
        up = [pltpu.roll(m[c][j], 7, 0) for j in range(4)] + [edge_hi]
        results = []
        for j in range(4):
            south = jnp.where(first_row, down[j], down[j + 1])
            north = jnp.where(last_row, up[j + 1], up[j])
            ends = pltpu.roll(col[pl.ds((c * 2 + half) * CY + 8 * j, 8), :], shift, 1)
            lower = jnp.where(first_lane, ends, pltpu.roll(m[c][j], 1, 1))
            upper = jnp.where(last_lane, ends, pltpu.roll(m[c][j], CZ - 1, 1))
            total = minus[0][j] * cells(c, ahead, j) + plus[0][j] * cells(c, behind, j)
            total = total + (minus[1][j] * north + plus[1][j] * south)
            total = total + (minus[2][j] * upper + plus[2][j] * lower)
            own = tables[pl.ds(64 + 8 * j, 8), :] if c < 2 else 4.0
            total = total + own * m[c][j]
            results.append(total * tables[pl.ds(32 + 8 * j, 8), :])
        for k in range(2):
            value = jnp.concatenate(results[2 * k : 2 * k + 2], axis=0).astype(BF16)
            stepped[pl.ds(pl.multiple_of((c * STATIONS + st) * CY + 16 * k, 16), 16), :] = value
            rounded[pl.ds((c * 16 + s) * CY + 16 * k, 16), :] = value.astype(F32)


def pool_slab(rounded, feat):
    residue = iota((8, 128), 1) % 4
    merged = [None] * 30

    def put(f, r, value, source):
        shift = (r - source) % 128
        value = pltpu.roll(value, shift, 1) if shift else value
        merged[f] = value if merged[f] is None else jnp.where(residue == r, value, merged[f])

    for r in range(4):
        sums = [[None] * 4 for _ in range(3)]
        products = [None] * 6
        for dx in range(4):
            for dy in range(4):
                q = (dx // 2) * 2 + dy // 2
                u = [rounded[pl.ds((c * 16 + 4 * r + dx) * CY + dy, 8, stride=4), :] for c in range(3)]
                for c in range(3):
                    sums[c][q] = u[c] if sums[c][q] is None else sums[c][q] + u[c]
                for k, (a, b) in enumerate(PAIRS):
                    value = u[a] * u[b]
                    products[k] = value if products[k] is None else products[k] + value
        means = []
        for c in range(3):
            point = None
            for q in range(4):
                two = sums[c][q] + pltpu.roll(sums[c][q], 127, 1)
                put(c * 8 + 2 * q, r, two, 0)
                put(c * 8 + 2 * q + 1, r, two, 2)
                point = two if point is None else point + two
            means.append((point + pltpu.roll(point, 126, 1)) * (1.0 / 64))
        for k, (a, b) in enumerate(PAIRS):
            two = products[k] + pltpu.roll(products[k], 127, 1)
            four = two + pltpu.roll(two, 126, 1)
            put(24 + k, r, four * (1.0 / 64) - means[a] * means[b], 0)
    for f in range(24):
        feat[pl.ds(8 * f, 8), :] = merged[f] * 0.125
    for f in range(24, 30):
        feat[pl.ds(8 * f, 8), :] = merged[f].astype(BF16).astype(F32)


def column_table(row):
    wide = jnp.broadcast_to(row, (128, HID))
    return jnp.concatenate([jnp.transpose(wide[:, :128]), jnp.transpose(wide[:, 128:])], axis=0)


def prepare_weights(w_in, b_in, w_mid, b_mid, w_out, b_out, win, wmid, wmid_t, wout, wout_t, bias_mid, bias_out, tmp):
    lane = iota((HID, 128), 1)
    bias = column_table(b_in[...]) * 0.5
    high = bias.astype(BF16).astype(F32)
    tmp[pl.ds(0, 128), :] = jnp.zeros((128, 128), F32)
    halves = []
    for h in range(2):
        tmp[pl.ds(0, 24), :] = w_in[:, 128 * h : 128 * h + 128].astype(F32) * 0.5
        halves.append(jnp.transpose(tmp[pl.ds(0, 128), :]))
    full = jnp.concatenate(halves, axis=0)
    full = jnp.where(lane == 30, high, jnp.where(lane == 31, bias - high, full))
    win[...] = full[:, 0:32].astype(BF16)
    mid = w_mid[...].astype(F32) * 0.5
    wmid[...] = mid.astype(BF16)
    wmid_t[...] = jnp.transpose(mid).astype(BF16)
    bias_mid[...] = column_table(b_mid[...]) * 0.5
    for h in range(2):
        tmp[pl.ds(0, 128), :] = jnp.zeros((128, 128), F32)
        tmp[pl.ds(0, 6), :] = w_out[:, 128 * h : 128 * h + 128].astype(F32)
        wout[:, 128 * h : 128 * h + 128] = tmp[pl.ds(0, 16), :].astype(BF16)
        wout_t[pl.ds(128 * h, 128), :] = (jnp.transpose(tmp[pl.ds(0, 128), :])[:, 0:16] * 0.5).astype(BF16)
    row = iota((8, 128), 0)
    table = jnp.where(row >= 6, 1.0, 0.0)
    for k in range(6):
        table = jnp.where(row == k, b_out[k], table)
    bias_out[...] = table


def widen(table, lanes):
    return jnp.concatenate([table] * (lanes // 128), axis=1)


def lane_sum(value):
    total = value[:, 0:128]
    for k in range(1, value.shape[1] // 128):
        total = total + value[:, 128 * k : 128 * k + 128]
    return total


def train_part(x, targets, win, wmid, wmid_t, wout, wout_t, bias_mid, bias_out, pred, g_in, g_mid, g_out, g_bmid, g_bout, g_loss):
    n = x.shape[1]
    h1 = jnp.dot(win[...], x, preferred_element_type=F32)
    t1 = jnp.tanh(h1)
    p1 = 1.0 + t1
    a1 = h1 * p1
    slope1 = p1 + a1 * (2.0 - p1)
    act1 = a1.astype(BF16)
    h2 = jnp.dot(wmid[...], act1, preferred_element_type=F32) + widen(bias_mid[...], n)
    p2 = 1.0 + jnp.tanh(h2)
    a2 = h2 * p2
    slope2 = p2 + a2 * (2.0 - p2)
    act2 = a2.astype(BF16)
    prediction = jnp.dot(wout[...], act2, preferred_element_type=F32)[0:8] + widen(bias_out[...], n)
    pred[...] = prediction
    residual = prediction - targets
    g_loss[...] += lane_sum(residual * residual)
    grad = (residual * (2.0 / (6 * SAMPLES))).astype(BF16).astype(F32)
    g_bout[...] += lane_sum(grad)
    grad = jnp.concatenate([grad, jnp.zeros_like(grad)], axis=0).astype(BF16)
    g_out[...] += lax.dot_general(grad, act2, NT, preferred_element_type=F32)
    d2 = jnp.dot(wout_t[...], grad, preferred_element_type=F32) * slope2
    g_bmid[...] += lane_sum(d2)
    grad2 = d2.astype(BF16)
    g_mid[...] += lax.dot_general(grad2, act1, NT, preferred_element_type=F32)
    d1 = jnp.dot(wmid_t[...], grad2, preferred_element_type=F32) * slope1
    grad1 = d1.astype(BF16)
    g_in[...] += lax.dot_general(grad1, x, NT, preferred_element_type=F32)


def scatter_slab(a, pred, table, ordered):
    lane = iota((8, 128), 1)
    point = lane % 64
    quarter = point // 4 % 4
    source = 4 * (point % 4) + point // 16
    low = lane < 64
    for b in range(2):
        blocks = [pred[:, 128 * (4 * b + q) : 128 * (4 * b + q) + 128] for q in range(4)]
        for c in range(8):
            index = source + 16 * c
            value = jnp.take_along_axis(blocks[0], index, axis=1)
            for q in range(1, 4):
                value = jnp.where(quarter == q, jnp.take_along_axis(blocks[q], index, axis=1), value)
            value = jnp.where(low, value, pltpu.roll(value, 5, 0))
            ordered[table[a, b, c]] = value[0:3]


def main_kernel(
    v, wall, hart, table, lo, hi, col, w_in, b_in, w_mid, b_mid, w_out, b_out,
    stepped_out, grads, ordered,
    stepped, rounded, tables, feat, xs, targets, pred, win, wmid, wmid_t, wout, wout_t, bias_mid, bias_out, tmp,
    g_in, g_mid, g_out, g_bmid, g_bout, g_loss, store,
):
    def store_copy(c, a):
        rows = pl.ds(pl.multiple_of(c * STATIONS * CY + a * 16 * CY, 16), 16 * CY)
        return pltpu.make_async_copy(stepped.at[rows], stepped_out.at[rows], store.at[c])

    fluid = (1 - wall[...]).astype(F32)
    tables[pl.ds(0, 32), :] = fluid
    tables[pl.ds(32, 32), :] = fluid * 0.1
    tables[pl.ds(64, 32), :] = 2.0 - 2.0 * hart[...].astype(F32)
    prepare_weights(w_in, b_in, w_mid, b_mid, w_out, b_out, win, wmid, wmid_t, wout, wout_t, bias_mid, bias_out, tmp)
    for ref in (g_in, g_mid, g_out, g_bmid, g_bout, g_loss):
        ref[...] = jnp.zeros_like(ref)
    feat[pl.ds(240, 16), :] = jnp.ones((16, 128), F32)

    def stencil_slab(a):
        def station(s):
            stencil_station(v, lo, hi, col, tables, stepped, rounded, a * 16 + s, s)

        for s in range(16):
            station(s)
        for c in range(3):
            store_copy(c, a).start()

    def samples(a):
        pool_slab(rounded, feat)
        for yp in range(8):
            lanes = slice(128 * yp, 128 * yp + 128)
            xs[:, lanes] = feat[pl.ds(yp, 32, stride=8), :].astype(BF16)
            targets[:, lanes] = feat[pl.ds(192 + yp, 8, stride=8), :]

    def train(a):
        train_part(
            xs[...], targets[...], win, wmid, wmid_t, wout, wout_t, bias_mid, bias_out,
            pred, g_in, g_mid, g_out, g_bmid, g_bout, g_loss,
        )
        scatter_slab(a, pred, table, ordered)

    def slab(a, carry):
        samples(a)
        train(a)
        stencil_slab(a + 1)
        return carry

    stencil_slab(0)
    lax.fori_loop(0, SLABS - 1, slab, 0)
    samples(SLABS - 1)
    train(SLABS - 1)
    for c in range(3):
        wait_bytes(stepped.at[pl.ds(0, STATIONS * CY)], store.at[c])
    for t in range(64):
        grads[t // 5, t % 5] = g_mid[pl.ds(8 * (t // 2), 8), 128 * (t % 2) : 128 * (t % 2) + 128]
    tmp[:, 0:32] = g_in[...]
    for h in range(2):
        turned = jnp.transpose(tmp[pl.ds(128 * h, 128), :])
        for k in range(4):
            t = 64 + 2 * k + h
            grads[t // 5, t % 5] = turned[8 * k : 8 * k + 8]
    row = iota((8, 128), 0)
    lane = iota((8, 128), 1)
    sums_out = jnp.sum(g_bout[...], axis=1, keepdims=True)
    last = jnp.sum(jnp.where((lane == row + 8) & (row < 6), sums_out, 0.0), axis=0, keepdims=True)
    loss = jnp.sum(jnp.sum(g_loss[...], axis=1, keepdims=True), axis=0, keepdims=True)
    last = jnp.where(lane[0:1] == 0, loss, last)
    for k in range(2):
        t = 72 + k
        bias = jnp.sum(jnp.transpose(g_bmid[pl.ds(128 * k, 128), :]), axis=0, keepdims=True)
        value = g_out[pl.ds(0, 8), 128 * k : 128 * k + 128]
        grads[t // 5, t % 5] = jnp.where(row == 6, bias, jnp.where(row == 7, last, value))
    for t in range(74, 80):
        grads[t // 5, t % 5] = jnp.zeros((8, 128), F32)


def main_call(vel, wall, hart, table, lo, hi, col, w_in, b_in, w_mid, b_mid, w_out, b_out):
    vm = pl.BlockSpec(memory_space=pltpu.VMEM)
    sm = pl.BlockSpec(memory_space=pltpu.SMEM)
    anywhere = pl.BlockSpec(memory_space=pl.ANY)
    return pl.pallas_call(
        main_kernel,
        name="step_train",
        out_shape=[
            jax.ShapeDtypeStruct((ROWS, 128), BF16),
            jax.ShapeDtypeStruct((16, 5, 8, 128), F32),
            jax.ShapeDtypeStruct((TILES, 3, 128), F32),
        ],
        in_specs=[vm, vm, vm, sm, vm, vm, vm, vm, vm, vm, vm, vm, sm],
        out_specs=[anywhere, vm, vm],
        scratch_shapes=[
            pltpu.VMEM((ROWS, 128), BF16),
            pltpu.VMEM((3 * 16 * CY, 128), F32),
            pltpu.VMEM((96, 128), F32),
            pltpu.VMEM((256, 128), F32),
            pltpu.VMEM((32, LANES), BF16),
            pltpu.VMEM((8, LANES), F32),
            pltpu.VMEM((8, LANES), F32),
            pltpu.VMEM((HID, 32), BF16),
            pltpu.VMEM((HID, HID), BF16),
            pltpu.VMEM((HID, HID), BF16),
            pltpu.VMEM((16, HID), BF16),
            pltpu.VMEM((HID, 16), BF16),
            pltpu.VMEM((HID, 128), F32),
            pltpu.VMEM((8, 128), F32),
            pltpu.VMEM((HID, 128), F32),
            pltpu.VMEM((HID, 32), F32),
            pltpu.VMEM((HID, HID), F32),
            pltpu.VMEM((16, HID), F32),
            pltpu.VMEM((HID, 128), F32),
            pltpu.VMEM((8, 128), F32),
            pltpu.VMEM((8, 128), F32),
            pltpu.SemaphoreType.DMA((3,)),
        ],
        compiler_params=pltpu.CompilerParams(vmem_limit_bytes=32 << 20),
    )(vel, wall, hart, table, lo, hi, col, w_in, b_in, w_mid, b_mid, w_out, b_out)


def share_kernel(
    g, p, total, got,
    part, mine, column, hop, s0, r0, s1, r1, s2, r2, s3, r3, s4, r4,
):
    y = lax.axis_index("gy")
    z = lax.axis_index("gz")
    barrier = pltpu.get_barrier_semaphore()
    for d in range(1, N_GY):
        pl.semaphore_signal(barrier, inc=1, device_id=((y + d) % N_GY, z), device_id_type=MESH)
    for d in range(1, N_GZ):
        pl.semaphore_signal(barrier, inc=1, device_id=(y, (z + d) % N_GZ), device_id_type=MESH)
    pl.semaphore_wait(barrier, N_GY + N_GZ - 2)

    def send(src, dst, ss, rs, qy, qz):
        pltpu.make_async_remote_copy(src, dst, ss, rs, device_id=(qy, qz), device_id_type=MESH).start()

    for d in range(1, N_GY):
        q = (y + d) % N_GY
        send(g.at[q], part.at[y], s0, r0, q, z)
    for d in range(1, N_GZ):
        q = (z + d) % N_GZ
        send(p.at[:, q], hop.at[z], s1, r1, y, q)
    hop[z] = p[:, z]
    part[y] = g[y]
    wait_bytes(part.at[pl.ds(0, N_GY - 1)], r0)
    column[z] = jnp.sum(part[...], axis=0)
    for d in range(1, N_GZ):
        q = (z + d) % N_GZ
        send(column.at[z], column.at[z], s2, r2, y, q)
    wait_bytes(hop.at[pl.ds(0, N_GZ - 1)], r1)
    for d in range(1, N_GY):
        q = (y + d) % N_GY
        send(hop.at[:, q], got.at[y], s3, r3, q, z)
    got[y] = hop[:, y]
    wait_bytes(column.at[pl.ds(0, N_GZ - 1)], r2)
    mine[...] = jnp.sum(column[...], axis=0)
    for d in range(1, N_GY):
        q = (y + d) % N_GY
        send(mine, total.at[y], s4, r4, q, z)
    total[y] = mine[...]
    wait_bytes(got.at[pl.ds(0, N_GY - 1)], r3)
    wait_bytes(total.at[pl.ds(0, N_GY - 1)], r4)
    wait_bytes(part.at[pl.ds(0, N_GY - 1)], s0)
    wait_bytes(hop.at[pl.ds(0, N_GZ - 1)], s1)
    wait_bytes(column.at[pl.ds(0, N_GZ - 1)], s2)
    wait_bytes(got.at[pl.ds(0, N_GY - 1)], s3)
    wait_bytes(total.at[pl.ds(0, N_GY - 1)], s4)


def share_call(grads, ordered):
    vm = pl.BlockSpec(memory_space=pltpu.VMEM)
    return pl.pallas_call(
        share_kernel,
        name="share",
        out_shape=[
            jax.ShapeDtypeStruct((N_GY, 5, 8, 128), F32),
            jax.ShapeDtypeStruct((N_GY, N_GZ, 3, 128), F32),
        ],
        in_specs=[vm, vm],
        out_specs=[vm] * 2,
        scratch_shapes=[
            pltpu.VMEM((N_GY, 5, 8, 128), F32),
            pltpu.VMEM((5, 8, 128), F32),
            pltpu.VMEM((N_GZ, 5, 8, 128), F32),
            pltpu.VMEM((N_GZ, N_GY, 3, 128), F32),
        ]
        + [pltpu.SemaphoreType.DMA] * 10,
        compiler_params=pltpu.CompilerParams(collective_id=1, has_side_effects=True, vmem_limit_bytes=16 << 20),
    )(grads, ordered)


def finish_kernel(total, got, pred_out, loss_out, in_out, bin_out, mid_out, bmid_out, out_out, bout_out):
    low = iota((3, 128), 1) < 64
    for j in range(TILES // 2):
        first = got[(2 * j) // N_GZ, (2 * j) % N_GZ]
        second = got[(2 * j + 1) // N_GZ, (2 * j + 1) % N_GZ]
        lanes = slice(128 * j, 128 * j + 128)
        pred_out[0:3, lanes] = jnp.where(low, first, pltpu.roll(second, 64, 1))
        pred_out[3:6, lanes] = jnp.where(low, pltpu.roll(first, 64, 1), second)
    for t in range(64):
        mid_out[pl.ds(8 * (t // 2), 8), 128 * (t % 2) : 128 * (t % 2) + 128] = total[t // 5, t % 5]
    for h in range(2):
        lanes = slice(128 * h, 128 * h + 128)
        for k in range(4):
            t = 64 + 2 * k + h
            if k < 3:
                in_out[pl.ds(8 * k, 8), lanes] = total[t // 5, t % 5]
            else:
                bin_out[:, lanes] = total[t // 5, t % 5][6:7]
        last = total[(72 + h) // 5, (72 + h) % 5]
        out_out[:, lanes] = last[0:6]
        bmid_out[:, lanes] = last[6:7]
        if h == 0:
            loss_out[...] = last[7:8, 0:1] * (1.0 / (6 * SAMPLES))
            bout_out[...] = pltpu.roll(last, 120, 1)[7:8, 0:6]


def finish_call(total, got):
    vm = pl.BlockSpec(memory_space=pltpu.VMEM)
    return pl.pallas_call(
        finish_kernel,
        name="finish",
        out_shape=[
            jax.ShapeDtypeStruct((6, 64 * 128), F32),
            jax.ShapeDtypeStruct((1, 1), F32),
            jax.ShapeDtypeStruct((24, HID), F32),
            jax.ShapeDtypeStruct((1, HID), F32),
            jax.ShapeDtypeStruct((HID, HID), F32),
            jax.ShapeDtypeStruct((1, HID), F32),
            jax.ShapeDtypeStruct((6, HID), F32),
            jax.ShapeDtypeStruct((1, 6), F32),
        ],
        in_specs=[vm, vm],
        out_specs=[vm] * 8,
        compiler_params=pltpu.CompilerParams(vmem_limit_bytes=16 << 20),
    )(total, got)


def on_device(velocity, wall_mask, hartmann_mask, tile_table, w_in, b_in, w_mid, b_mid, w_out, b_out):
    vel = velocity.reshape(ROWS, CZ)
    lo, hi, col = halo_call(vel, wall_mask)
    stepped, grads, ordered = main_call(
        vel, wall_mask, hartmann_mask, tile_table, lo, hi, col,
        w_in.T, b_in.reshape(1, HID), w_mid, b_mid.reshape(1, HID), w_out, b_out,
    )
    total, got = share_call(grads, ordered.reshape(N_GY, N_GZ, 3, 128))
    prediction, loss, grad_in, grad_bin, grad_mid, grad_bmid, grad_out, grad_bout = finish_call(total, got)
    return (
        stepped.reshape(3, STATIONS, CY, CZ),
        prediction,
        loss.reshape(()),
        grad_in.T,
        grad_bin.reshape(HID),
        grad_mid,
        grad_bmid.reshape(HID),
        grad_out,
        grad_bout.reshape(6),
    )


def solution(mesh):
    whole = P()
    in_specs = (P(None, None, "gy", "gz"), P("gy", "gz"), P("gy", "gz"), P(None, "gy", "gz")) + (whole,) * 6
    out_specs = (P(None, None, "gy", "gz"), P(None, ("gy", "gz"))) + (whole,) * 7
    return jax.shard_map(on_device, mesh=mesh, in_specs=in_specs, out_specs=out_specs, check_vma=False)
```

```python
import functools

import jax
import jax.numpy as jnp
from jax import lax
from jax.experimental import pallas as pl
from jax.experimental.pallas import tpu as pltpu
from jax.sharding import PartitionSpec as P

MESH = pl.DeviceIdType.MESH
STATIONS = 128
CY = 32
CZ = 128
HID = 256
N_GY = 16
N_GZ = 8
TILES = 128
SAMPLES = 1048576
ROWS = 3 * STATIONS * CY
SLABS = 8
VMEM_LIMIT = 56
MOVES = 8
LANES = 1024
F32 = jnp.float32
BF16 = jnp.bfloat16
PAIRS = ((0, 0), (1, 1), (2, 2), (0, 1), (0, 2), (1, 2))
NT = (((1,), (1,)), ((), ()))


def iota(shape, dim):
    return lax.broadcasted_iota(jnp.int32, shape, dim)


def wait_bytes(ref, sem):
    pltpu.make_async_copy(ref, ref, sem).wait()


def column_table(row):
    wide = jnp.broadcast_to(row, (128, HID))
    return jnp.concatenate([jnp.transpose(wide[:, :128]), jnp.transpose(wide[:, 128:])], axis=0)


def prepare_weights(w_in, b_in, w_mid, b_mid, w_out, b_out, win, wmid, wmid_t, wout, wout_t, bias_mid, bias_out, tmp):
    lane = iota((HID, 128), 1)
    bias = column_table(b_in[...]) * 0.5
    high = bias.astype(BF16).astype(F32)
    tmp[pl.ds(0, 128), :] = jnp.zeros((128, 128), F32)
    halves = []
    for h in range(2):
        tmp[pl.ds(0, 24), :] = w_in[:, 128 * h : 128 * h + 128].astype(F32) * 0.5
        halves.append(jnp.transpose(tmp[pl.ds(0, 128), :]))
    full = jnp.concatenate(halves, axis=0)
    full = jnp.where(lane == 30, high, jnp.where(lane == 31, bias - high, full))
    win[...] = full[:, 0:32].astype(BF16)
    mid = w_mid[...].astype(F32) * 0.5
    wmid[...] = mid.astype(BF16)
    wmid_t[...] = jnp.transpose(mid).astype(BF16)
    bias_mid[...] = column_table(b_mid[...]) * 0.5
    for h in range(2):
        tmp[pl.ds(0, 128), :] = jnp.zeros((128, 128), F32)
        tmp[pl.ds(0, 6), :] = w_out[:, 128 * h : 128 * h + 128].astype(F32)
        wout[:, 128 * h : 128 * h + 128] = tmp[pl.ds(0, 16), :].astype(BF16)
        wout_t[pl.ds(128 * h, 128), :] = (jnp.transpose(tmp[pl.ds(0, 128), :])[:, 0:16] * 0.5).astype(BF16)
    row = iota((8, 128), 0)
    table = jnp.where(row >= 6, 1.0, 0.0)
    tmp[pl.ds(0, 1), 0:6] = b_out[...]
    wide = jnp.broadcast_to(tmp[pl.ds(0, 1), :], (128, 128))
    bias_out[...] = jnp.where(row < 6, jnp.transpose(wide)[0:8], table)


def pack_edges(v, fluid, edge_lo, edge_hi, c):
    first = c * STATIONS * CY
    rows = pl.ds(c * STATIONS, STATIONS)
    edge_lo[rows, :] = (v[pl.ds(first, STATIONS, stride=CY), :] * fluid[0:1, :]).astype(BF16)
    edge_hi[rows, :] = (v[pl.ds(first + CY - 1, STATIONS, stride=CY), :] * fluid[CY - 1 : CY, :]).astype(BF16)


def pack_columns(v, fluid, to_left, to_right, c):
    pair = iota((8, 128), 1) // 2
    odd = iota((8, 128), 1) % 2 == 1
    def station(s, acc):
        here = pair == s
        out = []
        for h in range(2):
            for j in range(4):
                cells = v[pl.ds((c * STATIONS + h * 64 + s) * CY + 8 * j, 8), :]
                out.append(jnp.where(here, pltpu.roll(cells, 2 * s + 1, 1), acc[len(out)]))
        return tuple(out)

    packed = lax.fori_loop(0, 64, station, tuple(jnp.zeros((8, 128), F32) for _ in range(8)), unroll=8)
    for k in range(2):
        left, right = [], []
        for j in (2 * k, 2 * k + 1):
            mask = fluid[8 * j : 8 * j + 8, :]
            near, far = packed[j], packed[4 + j]
            right.append(jnp.where(odd, pltpu.roll(far, 1, 1), near) * mask[:, CZ - 1 : CZ])
            left.append(jnp.where(odd, far, pltpu.roll(near, 127, 1)) * mask[:, 0:1])
        rows = pl.ds(c * CY + 16 * k, 16)
        to_right[rows, :] = jnp.concatenate(right, axis=0).astype(BF16)
        to_left[rows, :] = jnp.concatenate(left, axis=0).astype(BF16)


def stencil_station(v, lo, hi, col, tables, stepped, rounded, st, s):
    ahead = lax.rem(st + 1, STATIONS)
    behind = lax.rem(st + STATIONS - 1, STATIONS)
    half = st // 64
    shift = 126 - 2 * lax.rem(st, 64)
    first_row = iota((8, 128), 0) == 0
    last_row = iota((8, 128), 0) == 7
    first_lane = iota((8, 128), 1) == 0
    last_lane = iota((8, 128), 1) == CZ - 1

    def cells(c, t, j):
        return v[pl.ds((c * STATIONS + t) * CY + 8 * j, 8), :]

    m = [[cells(c, st, j) * tables[pl.ds(8 * j, 8), :] for j in range(4)] for c in range(3)]
    minus = [[1.0 - m[c][j] for j in range(4)] for c in range(3)]
    plus = [[1.0 + m[c][j] for j in range(4)] for c in range(3)]
    for c in range(3):
        edge_lo = jnp.broadcast_to(lo[pl.ds(c * STATIONS + st, 1), :], (8, 128))
        edge_hi = jnp.broadcast_to(hi[pl.ds(c * STATIONS + st, 1), :], (8, 128))
        down = [edge_lo] + [pltpu.roll(m[c][j], 1, 0) for j in range(4)]
        up = [pltpu.roll(m[c][j], 7, 0) for j in range(4)] + [edge_hi]
        results = []
        for j in range(4):
            south = jnp.where(first_row, down[j], down[j + 1])
            north = jnp.where(last_row, up[j + 1], up[j])
            ends = pltpu.roll(col[pl.ds((c * 2 + half) * CY + 8 * j, 8), :], shift, 1)
            lower = jnp.where(first_lane, ends, pltpu.roll(m[c][j], 1, 1))
            upper = jnp.where(last_lane, ends, pltpu.roll(m[c][j], CZ - 1, 1))
            total = minus[0][j] * cells(c, ahead, j) + plus[0][j] * cells(c, behind, j)
            total = total + (minus[1][j] * north + plus[1][j] * south)
            total = total + (minus[2][j] * upper + plus[2][j] * lower)
            own = tables[pl.ds(64 + 8 * j, 8), :] if c < 2 else 4.0
            total = total + own * m[c][j]
            results.append(total * tables[pl.ds(32 + 8 * j, 8), :])
        for k in range(2):
            value = jnp.concatenate(results[2 * k : 2 * k + 2], axis=0).astype(BF16)
            stepped[pl.ds(pl.multiple_of((c * STATIONS + st) * CY + 16 * k, 16), 16), :] = value
            rounded[pl.ds((c * 16 + s) * CY + 16 * k, 16), :] = value.astype(F32)


def pool_slab(rounded, feat):
    residue = iota((8, 128), 1) % 4
    merged = [None] * 30

    def put(f, r, value, source):
        shift = (r - source) % 128
        value = pltpu.roll(value, shift, 1) if shift else value
        merged[f] = value if merged[f] is None else jnp.where(residue == r, value, merged[f])

    for r in range(4):
        sums = [[None] * 4 for _ in range(3)]
        products = [None] * 6
        for dx in range(4):
            for dy in range(4):
                q = (dx // 2) * 2 + dy // 2
                u = [rounded[pl.ds((c * 16 + 4 * r + dx) * CY + dy, 8, stride=4), :] for c in range(3)]
                for c in range(3):
                    sums[c][q] = u[c] if sums[c][q] is None else sums[c][q] + u[c]
                for k, (a, b) in enumerate(PAIRS):
                    value = u[a] * u[b]
                    products[k] = value if products[k] is None else products[k] + value
        means = []
        for c in range(3):
            point = None
            for q in range(4):
                two = sums[c][q] + pltpu.roll(sums[c][q], 127, 1)
                put(c * 8 + 2 * q, r, two, 0)
                put(c * 8 + 2 * q + 1, r, two, 2)
                point = two if point is None else point + two
            means.append((point + pltpu.roll(point, 126, 1)) * (1.0 / 64))
        for k, (a, b) in enumerate(PAIRS):
            two = products[k] + pltpu.roll(products[k], 127, 1)
            four = two + pltpu.roll(two, 126, 1)
            put(24 + k, r, four * (1.0 / 64) - means[a] * means[b], 0)
    for f in range(24):
        feat[pl.ds(8 * f, 8), :] = merged[f] * 0.125
    for f in range(24, 30):
        feat[pl.ds(8 * f, 8), :] = merged[f].astype(BF16).astype(F32)


def widen(table, lanes):
    return jnp.concatenate([table] * (lanes // 128), axis=1)


def lane_sum(value):
    total = value[:, 0:128]
    for k in range(1, value.shape[1] // 128):
        total = total + value[:, 128 * k : 128 * k + 128]
    return total


def train_part(x, targets, win, wmid, wmid_t, wout, wout_t, bias_mid, bias_out, pred, g_in, g_mid, g_out, g_bmid, g_bout, g_loss):
    n = x.shape[1]
    h1 = jnp.dot(win[...], x, preferred_element_type=F32)
    t1 = jnp.tanh(h1)
    p1 = 1.0 + t1
    a1 = h1 * p1
    slope1 = p1 + a1 * (2.0 - p1)
    act1 = a1.astype(BF16)
    h2 = jnp.dot(wmid[...], act1, preferred_element_type=F32) + widen(bias_mid[...], n)
    p2 = 1.0 + jnp.tanh(h2)
    a2 = h2 * p2
    slope2 = p2 + a2 * (2.0 - p2)
    act2 = a2.astype(BF16)
    prediction = jnp.dot(wout[...], act2, preferred_element_type=F32)[0:8] + widen(bias_out[...], n)
    pred[...] = prediction
    residual = prediction - targets
    g_loss[...] += lane_sum(residual * residual)
    grad = (residual * (2.0 / (6 * SAMPLES))).astype(BF16).astype(F32)
    g_bout[...] += lane_sum(grad)
    grad = jnp.concatenate([grad, jnp.zeros_like(grad)], axis=0).astype(BF16)
    g_out[...] += lax.dot_general(grad, act2, NT, preferred_element_type=F32)
    d2 = jnp.dot(wout_t[...], grad, preferred_element_type=F32) * slope2
    g_bmid[...] += lane_sum(d2)
    grad2 = d2.astype(BF16)
    g_mid[...] += lax.dot_general(grad2, act1, NT, preferred_element_type=F32)
    d1 = jnp.dot(wmid_t[...], grad2, preferred_element_type=F32) * slope1
    grad1 = d1.astype(BF16)
    g_in[...] += lax.dot_general(grad1, x, NT, preferred_element_type=F32)


def keep_predictions(a, pred, tiles):
    lane = iota((8, 128), 1)
    point = lane % 64
    quarter = point // 4 % 4
    source = 4 * (point % 4) + point // 16
    low = lane < 64
    for b in range(2):
        blocks = [pred[:, 128 * (4 * b + q) : 128 * (4 * b + q) + 128] for q in range(4)]
        for c in range(8):
            index = source + 16 * c
            value = jnp.take_along_axis(blocks[0], index, axis=1)
            for q in range(1, 4):
                value = jnp.where(quarter == q, jnp.take_along_axis(blocks[q], index, axis=1), value)
            value = jnp.where(low, value, pltpu.roll(value, 5, 0))
            for k in range(3):
                tiles[pl.ds(k * TILES + a * 16 + b * 8 + c, 1), :] = value[k : k + 1]


def order_tiles(table, row, tiles, ordered):
    for a in range(8):
        for b in range(2):
            first = a * 16 + b * 8
            row[0:1, first : first + 8] = table[a, b : b + 1, :]
    place = iota((TILES, 128), 0)
    slot = place % N_GY * N_GZ + place // N_GY
    chosen = jnp.where(jnp.broadcast_to(row[0:1, :], (TILES, 128)) == slot, 1.0, 0.0).astype(BF16)
    for k in range(3):
        value = tiles[pl.ds(k * TILES, TILES), :]
        high = value.astype(BF16)
        rest = value - high.astype(F32)
        middle = rest.astype(BF16)
        last = (rest - middle.astype(F32)).astype(BF16)
        total = jnp.dot(chosen, high, preferred_element_type=F32)
        total = total + jnp.dot(chosen, middle, preferred_element_type=F32)
        total = total + jnp.dot(chosen, last, preferred_element_type=F32)
        ordered[:, k, :] = total


def pack_gradients(g_in, g_mid, g_out, g_bmid, g_bout, g_loss, tmp, grads):
    for t in range(64):
        grads[t // 5, t % 5] = g_mid[pl.ds(8 * (t // 2), 8), 128 * (t % 2) : 128 * (t % 2) + 128]
    tmp[:, 0:32] = g_in[...]
    for h in range(2):
        turned = jnp.transpose(tmp[pl.ds(128 * h, 128), :])
        for k in range(4):
            t = 64 + 2 * k + h
            grads[t // 5, t % 5] = turned[8 * k : 8 * k + 8]
    row = iota((8, 128), 0)
    lane = iota((8, 128), 1)
    sums_out = jnp.sum(g_bout[...], axis=1, keepdims=True)
    last = jnp.sum(jnp.where((lane == row + 8) & (row < 6), sums_out, 0.0), axis=0, keepdims=True)
    loss = jnp.sum(jnp.sum(g_loss[...], axis=1, keepdims=True), axis=0, keepdims=True)
    last = jnp.where(lane[0:1] == 0, loss, last)
    for k in range(2):
        t = 72 + k
        bias = jnp.sum(jnp.transpose(g_bmid[pl.ds(128 * k, 128), :]), axis=0, keepdims=True)
        value = g_out[pl.ds(0, 8), 128 * k : 128 * k + 128]
        grads[t // 5, t % 5] = jnp.where(row == 6, bias, jnp.where(row == 7, last, value))
    for t in range(74, 80):
        grads[t // 5, t % 5] = jnp.zeros((8, 128), F32)


def whole_kernel(
    vel, wall_any, hart_any, table_any, w_in_any, b_in_any, w_mid_any, b_mid_any, w_out_any, b_out_any,
    stepped_out, total, got,
    v, wall, hart, table, w_in, b_in, w_mid, b_mid, w_out, b_out,
    win, wmid, wmid_t, wout, wout_t, bias_mid, bias_out, tmp, row,
    edge_lo, edge_hi, to_left, to_right, got_lo, got_hi, got_left, got_right, lo, hi, col,
    stepped, rounded, tables, feat, xs, targets, pred, tiles, ordered,
    g_in, g_mid, g_out, g_bmid, g_bout, g_loss, grads, part, mine, column, hop,
    load, send_halo, recv_halo, store, s0, r0, s1, r1, s2, r2, s3, r3, s4, r4,
):
    y = lax.axis_index("gy")
    z = lax.axis_index("gz")
    slabs = [pl.ds(c * STATIONS * CY, STATIONS * CY) for c in range(3)]
    loads = [pltpu.make_async_copy(wall_any, wall, load.at[0])]
    loads += [pltpu.make_async_copy(vel.at[slabs[c]], v.at[slabs[c]], load.at[1 + c]) for c in range(3)]
    pairs = (
        (w_in_any, w_in), (b_in_any, b_in), (w_mid_any, w_mid), (b_mid_any, b_mid),
        (w_out_any, w_out), (b_out_any, b_out), (hart_any, hart), (table_any, table),
    )
    loads += [pltpu.make_async_copy(src, dst, load.at[4 + k]) for k, (src, dst) in enumerate(pairs)]
    for copy in loads:
        copy.start()

    barrier = pltpu.get_barrier_semaphore()
    for d in range(1, N_GY):
        pl.semaphore_signal(barrier, inc=1, device_id=((y + d) % N_GY, z), device_id_type=MESH)
    for d in range(1, N_GZ):
        pl.semaphore_signal(barrier, inc=1, device_id=(y, (z + d) % N_GZ), device_id_type=MESH)

    loads[0].wait()
    fluid = (1 - wall[...]).astype(F32)
    tables[pl.ds(0, 32), :] = fluid
    tables[pl.ds(32, 32), :] = fluid * 0.1
    for c in range(3):
        loads[1 + c].wait()
        pack_columns(v, tables, to_left, to_right, c)
        pack_edges(v, tables, edge_lo, edge_hi, c)
    pl.semaphore_wait(barrier, N_GY + N_GZ - 2)
    below = ((y + N_GY - 1) % N_GY, z)
    above = ((y + 1) % N_GY, z)
    left = (y, (z + N_GZ - 1) % N_GZ)
    right = (y, (z + 1) % N_GZ)
    copies = []
    for k, (src, dst, peer) in enumerate(
        ((to_left, got_right, left), (to_right, got_left, right), (edge_lo, got_hi, below), (edge_hi, got_lo, above))
    ):
        copy = pltpu.make_async_remote_copy(
            src, dst, send_halo.at[k], recv_halo.at[k], device_id=peer, device_id_type=MESH
        )
        copy.start()
        copies.append(copy)
    for copy in loads[4:]:
        copy.wait()
    tables[pl.ds(64, 32), :] = 2.0 - 2.0 * hart[...].astype(F32)
    prepare_weights(w_in, b_in, w_mid, b_mid, w_out, b_out, win, wmid, wmid_t, wout, wout_t, bias_mid, bias_out, tmp)
    for ref in (g_in, g_mid, g_out, g_bmid, g_bout, g_loss):
        ref[...] = jnp.zeros_like(ref)
    feat[pl.ds(240, 16), :] = jnp.ones((16, 128), F32)
    for copy in copies:
        copy.wait_recv()
    lo[...] = got_lo[...].astype(F32) * jnp.where(y > 0, 1.0, 0.0)
    hi[...] = got_hi[...].astype(F32) * jnp.where(y < N_GY - 1, 1.0, 0.0)
    has_left = jnp.where(z > 0, 1.0, 0.0)
    has_right = jnp.where(z < N_GZ - 1, 1.0, 0.0)
    odd = iota((16, 128), 1) % 2 == 1
    for c in range(3):
        for k in range(2):
            rows = pl.ds(c * CY + 16 * k, 16)
            lower = got_left[rows, :].astype(F32) * has_left
            upper = got_right[rows, :].astype(F32) * has_right
            near = jnp.where(odd, pltpu.roll(upper, 1, 1), pltpu.roll(lower, 2, 1))
            far = jnp.where(odd, upper, pltpu.roll(lower, 1, 1))
            col[pl.ds((c * 2) * CY + 16 * k, 16), :] = near
            col[pl.ds((c * 2 + 1) * CY + 16 * k, 16), :] = far

    def store_copy(c, a):
        rows = pl.ds(pl.multiple_of(c * STATIONS * CY + a * 16 * CY, 16), 16 * CY)
        return pltpu.make_async_copy(stepped.at[rows], stepped_out.at[rows], store.at[c])

    def stencil_slab(a, unroll):
        def station(s, inner):
            stencil_station(v, lo, hi, col, tables, stepped, rounded, a * 16 + s, s)
            return inner

        lax.fori_loop(0, 16, station, 0, unroll=unroll)
        for c in range(3):
            store_copy(c, a).start()

    def samples():
        pool_slab(rounded, feat)
        for yp in range(8):
            lanes = slice(128 * yp, 128 * yp + 128)
            xs[:, lanes] = feat[pl.ds(yp, 32, stride=8), :].astype(BF16)
            targets[:, lanes] = feat[pl.ds(192 + yp, 8, stride=8), :]

    def train(a):
        train_part(
            xs[...], targets[...], win, wmid, wmid_t, wout, wout_t, bias_mid, bias_out,
            pred, g_in, g_mid, g_out, g_bmid, g_bout, g_loss,
        )
        keep_predictions(a, pred, tiles)

    def slab(a, carry):
        samples()
        train(a)
        stencil_slab(a + 1, 16)
        return carry

    stencil_slab(0, 4)
    lax.fori_loop(0, SLABS - 1, slab, 0)
    samples()
    train(SLABS - 1)
    pack_gradients(g_in, g_mid, g_out, g_bmid, g_bout, g_loss, tmp, grads)

    def send(src, dst, ss, rs, qy, qz):
        pltpu.make_async_remote_copy(src, dst, ss, rs, device_id=(qy, qz), device_id_type=MESH).start()

    for d in range(1, N_GY):
        q = (y + d) % N_GY
        send(grads.at[q], part.at[y], s0, r0, q, z)
    order_tiles(table, row, tiles, ordered)
    for d in range(1, N_GZ):
        q = (z + d) % N_GZ
        send(ordered.at[pl.ds(q * N_GY, N_GY)], hop.at[z], s1, r1, y, q)
    hop[z] = ordered[pl.ds(z * N_GY, N_GY)]
    part[y] = grads[y]
    wait_bytes(part.at[pl.ds(0, N_GY - 1)], r0)
    column[z] = jnp.sum(part[...], axis=0)
    for d in range(1, N_GZ):
        q = (z + d) % N_GZ
        send(column.at[z], column.at[z], s2, r2, y, q)
    wait_bytes(hop.at[pl.ds(0, N_GZ - 1)], r1)
    for d in range(1, N_GY):
        q = (y + d) % N_GY
        send(hop.at[:, q], got.at[y], s3, r3, q, z)
    got[y] = hop[:, y]
    wait_bytes(column.at[pl.ds(0, N_GZ - 1)], r2)
    mine[...] = jnp.sum(column[...], axis=0)
    for d in range(1, N_GY):
        q = (y + d) % N_GY
        send(mine, total.at[y], s4, r4, q, z)
    total[y] = mine[...]
    for c in range(3):
        wait_bytes(stepped.at[slabs[c]], store.at[c])
    for copy in copies:
        copy.wait_send()
    wait_bytes(got.at[pl.ds(0, N_GY - 1)], r3)
    wait_bytes(total.at[pl.ds(0, N_GY - 1)], r4)
    wait_bytes(part.at[pl.ds(0, N_GY - 1)], s0)
    wait_bytes(hop.at[pl.ds(0, N_GZ - 1)], s1)
    wait_bytes(column.at[pl.ds(0, N_GZ - 1)], s2)
    wait_bytes(got.at[pl.ds(0, N_GY - 1)], s3)
    wait_bytes(total.at[pl.ds(0, N_GY - 1)], s4)


def whole_call(*arrays):
    vm = pl.BlockSpec(memory_space=pltpu.VMEM)
    anywhere = pl.BlockSpec(memory_space=pl.ANY)
    i32 = jnp.int32
    scratch = [
        ((ROWS, 128), F32), ((CY, 128), i32), ((CY, 128), i32), ((8, 2, 8), i32), ((24, HID), BF16), ((1, HID), F32),
        ((HID, HID), BF16), ((1, HID), F32), ((6, HID), BF16), ((1, 6), F32),
        ((HID, 32), BF16), ((HID, HID), BF16), ((HID, HID), BF16), ((16, HID), BF16), ((HID, 16), BF16),
        ((HID, 128), F32), ((8, 128), F32), ((HID, 128), F32), ((8, 128), i32),
        ((384, 128), BF16), ((384, 128), BF16), ((96, 128), BF16), ((96, 128), BF16),
        ((384, 128), BF16), ((384, 128), BF16), ((96, 128), BF16), ((96, 128), BF16),
        ((384, 128), F32), ((384, 128), F32), ((192, 128), F32),
        ((ROWS, 128), BF16), ((3 * 16 * CY, 128), F32), ((96, 128), F32), ((256, 128), F32),
        ((32, LANES), BF16), ((8, LANES), F32), ((8, LANES), F32), ((3 * TILES, 128), F32), ((TILES, 3, 128), F32),
        ((HID, 32), F32), ((HID, HID), F32), ((16, HID), F32), ((HID, 128), F32), ((8, 128), F32), ((8, 128), F32),
        ((N_GY, 5, 8, 128), F32), ((N_GY, 5, 8, 128), F32), ((5, 8, 128), F32), ((N_GZ, 5, 8, 128), F32),
        ((N_GZ, N_GY, 3, 128), F32),
    ]
    dma = pltpu.SemaphoreType.DMA
    return pl.pallas_call(
        whole_kernel,
        name="whole",
        out_shape=[
            jax.ShapeDtypeStruct((ROWS, 128), BF16),
            jax.ShapeDtypeStruct((N_GY, 5, 8, 128), F32),
            jax.ShapeDtypeStruct((N_GY, N_GZ, 3, 128), F32),
        ],
        in_specs=[anywhere] * 10,
        out_specs=[anywhere, vm, vm],
        scratch_shapes=[pltpu.VMEM(shape, kind) for shape, kind in scratch] + [dma((12,)), dma((4,)), dma((4,)), dma((3,))] + [dma] * 10,
        compiler_params=pltpu.CompilerParams(collective_id=0, has_side_effects=True, vmem_limit_bytes=VMEM_LIMIT << 20),
    )(*arrays)


def finish_kernel(
    stepped_any, total_any, got_any,
    stepped_out, pred_out, loss_out, in_out, bin_out, mid_out, bmid_out, out_out, bout_out,
    held, total, got, load, take, give,
):
    fetch_got = pltpu.make_async_copy(got_any, got, load.at[0])
    fetch_total = pltpu.make_async_copy(total_any, total, load.at[1])
    fetch_got.start()
    fetch_total.start()
    count = ROWS // MOVES
    parts = [pl.ds(k * count, count) for k in range(MOVES)]
    takes = [pltpu.make_async_copy(stepped_any.at[parts[k]], held.at[parts[k]], take.at[k]) for k in range(MOVES)]
    gives = [pltpu.make_async_copy(held.at[parts[k]], stepped_out.at[parts[k]], give.at[k]) for k in range(MOVES)]
    for copy in takes:
        copy.start()
    for k in range(MOVES):
        takes[k].wait()
        gives[k].start()
    fetch_got.wait()
    low = iota((3, 128), 1) < 64
    for j in range(TILES // 2):
        first = got[(2 * j) // N_GZ, (2 * j) % N_GZ]
        second = got[(2 * j + 1) // N_GZ, (2 * j + 1) % N_GZ]
        lanes = slice(128 * j, 128 * j + 128)
        pred_out[0:3, lanes] = jnp.where(low, first, pltpu.roll(second, 64, 1))
        pred_out[3:6, lanes] = jnp.where(low, pltpu.roll(first, 64, 1), second)
    fetch_total.wait()
    for t in range(64):
        mid_out[pl.ds(8 * (t // 2), 8), 128 * (t % 2) : 128 * (t % 2) + 128] = total[t // 5, t % 5]
    for h in range(2):
        lanes = slice(128 * h, 128 * h + 128)
        for k in range(4):
            t = 64 + 2 * k + h
            if k < 3:
                in_out[pl.ds(8 * k, 8), lanes] = total[t // 5, t % 5]
            else:
                bin_out[:, lanes] = total[t // 5, t % 5][6:7]
        last = total[(72 + h) // 5, (72 + h) % 5]
        out_out[:, lanes] = last[0:6]
        bmid_out[:, lanes] = last[6:7]
        if h == 0:
            loss_out[...] = last[7:8, 0:1] * (1.0 / (6 * SAMPLES))
            bout_out[...] = pltpu.roll(last, 120, 1)[7:8, 0:6]
    for copy in gives:
        copy.wait()


def finish_call(stepped, total, got):
    anywhere = pl.BlockSpec(memory_space=pl.ANY)
    vm = pl.BlockSpec(memory_space=pltpu.VMEM)
    return pl.pallas_call(
        finish_kernel,
        name="finish",
        out_shape=[
            jax.ShapeDtypeStruct((ROWS, 128), BF16),
            jax.ShapeDtypeStruct((6, 64 * 128), F32),
            jax.ShapeDtypeStruct((1, 1), F32),
            jax.ShapeDtypeStruct((24, HID), F32),
            jax.ShapeDtypeStruct((1, HID), F32),
            jax.ShapeDtypeStruct((HID, HID), F32),
            jax.ShapeDtypeStruct((1, HID), F32),
            jax.ShapeDtypeStruct((6, HID), F32),
            jax.ShapeDtypeStruct((1, 6), F32),
        ],
        in_specs=[anywhere] * 3,
        out_specs=[anywhere] + [vm] * 8,
        scratch_shapes=[
            pltpu.VMEM((ROWS, 128), BF16),
            pltpu.VMEM((N_GY, 5, 8, 128), F32),
            pltpu.VMEM((N_GY, N_GZ, 3, 128), F32),
            pltpu.SemaphoreType.DMA((2,)),
            pltpu.SemaphoreType.DMA((MOVES,)),
            pltpu.SemaphoreType.DMA((MOVES,)),
        ],
        compiler_params=pltpu.CompilerParams(vmem_limit_bytes=VMEM_LIMIT << 20),
    )(stepped, total, got)


def on_device(velocity, wall_mask, hartmann_mask, tile_table, w_in, b_in, w_mid, b_mid, w_out, b_out):
    stepped, total, got = whole_call(
        velocity.reshape(ROWS, CZ), wall_mask, hartmann_mask, tile_table,
        w_in.T, b_in.reshape(1, HID), w_mid, b_mid.reshape(1, HID), w_out, b_out.reshape(1, 6),
    )
    stepped, prediction, loss, grad_in, grad_bin, grad_mid, grad_bmid, grad_out, grad_bout = finish_call(stepped, total, got)
    return (
        stepped.reshape(3, STATIONS, CY, CZ),
        prediction,
        loss.reshape(()),
        grad_in.T,
        grad_bin.reshape(HID),
        grad_mid,
        grad_bmid.reshape(HID),
        grad_out,
        grad_bout.reshape(6),
    )


def solution(mesh):
    whole = P()
    in_specs = (P(None, None, "gy", "gz"), P("gy", "gz"), P("gy", "gz"), P(None, "gy", "gz")) + (whole,) * 6
    out_specs = (P(None, None, "gy", "gz"), P(None, ("gy", "gz"))) + (whole,) * 7
    return jax.shard_map(on_device, mesh=mesh, in_specs=in_specs, out_specs=out_specs, check_vma=False)
```

```python
import functools

import jax
import jax.numpy as jnp
from jax import lax
from jax.experimental import pallas as pl
from jax.experimental.pallas import tpu as pltpu
from jax.sharding import PartitionSpec as P

MESH = pl.DeviceIdType.MESH
STATIONS = 128
CY = 32
CZ = 128
HID = 256
N_GY = 16
N_GZ = 8
TILES = 128
SAMPLES = 1048576
ROWS = 3 * STATIONS * CY
SLABS = 8
VMEM_LIMIT = 56
MOVES = 4
LANES = 1024
F32 = jnp.float32
BF16 = jnp.bfloat16
PAIRS = ((0, 0), (1, 1), (2, 2), (0, 1), (0, 2), (1, 2))
NT = (((1,), (1,)), ((), ()))


def iota(shape, dim):
    return lax.broadcasted_iota(jnp.int32, shape, dim)


def wait_bytes(ref, sem):
    pltpu.make_async_copy(ref, ref, sem).wait()


def column_table(row):
    wide = jnp.broadcast_to(row, (128, HID))
    return jnp.concatenate([jnp.transpose(wide[:, :128]), jnp.transpose(wide[:, 128:])], axis=0)


def prepare_weights(w_in, b_in, w_mid, b_mid, w_out, b_out, win, wmid, wmid_t, wout, wout_t, bias_mid, bias_out, tmp):
    lane = iota((HID, 128), 1)
    bias = column_table(b_in[...]) * 0.5
    high = bias.astype(BF16).astype(F32)
    tmp[pl.ds(0, 128), :] = jnp.zeros((128, 128), F32)
    halves = []
    for h in range(2):
        tmp[pl.ds(0, 24), :] = w_in[:, 128 * h : 128 * h + 128].astype(F32) * 0.5
        halves.append(jnp.transpose(tmp[pl.ds(0, 128), :]))
    full = jnp.concatenate(halves, axis=0)
    full = jnp.where(lane == 30, high, jnp.where(lane == 31, bias - high, full))
    win[...] = full[:, 0:32].astype(BF16)
    mid = w_mid[...].astype(F32) * 0.5
    wmid[...] = mid.astype(BF16)
    wmid_t[...] = jnp.transpose(mid).astype(BF16)
    bias_mid[...] = column_table(b_mid[...]) * 0.5
    for h in range(2):
        tmp[pl.ds(0, 128), :] = jnp.zeros((128, 128), F32)
        tmp[pl.ds(0, 6), :] = w_out[:, 128 * h : 128 * h + 128].astype(F32)
        wout[:, 128 * h : 128 * h + 128] = tmp[pl.ds(0, 16), :].astype(BF16)
        wout_t[pl.ds(128 * h, 128), :] = (jnp.transpose(tmp[pl.ds(0, 128), :])[:, 0:16] * 0.5).astype(BF16)
    row = iota((8, 128), 0)
    table = jnp.where(row >= 6, 1.0, 0.0)
    tmp[pl.ds(0, 1), 0:6] = b_out[...]
    wide = jnp.broadcast_to(tmp[pl.ds(0, 1), :], (128, 128))
    bias_out[...] = jnp.where(row < 6, jnp.transpose(wide)[0:8], table)


def pack_edges(v, fluid, edge_lo, edge_hi, c):
    first = c * STATIONS * CY
    rows = pl.ds(c * STATIONS, STATIONS)
    edge_lo[rows, :] = (v[pl.ds(first, STATIONS, stride=CY), :] * fluid[0:1, :]).astype(BF16)
    edge_hi[rows, :] = (v[pl.ds(first + CY - 1, STATIONS, stride=CY), :] * fluid[CY - 1 : CY, :]).astype(BF16)


def pack_columns(v, fluid, to_left, to_right, c):
    pair = iota((8, 128), 1) // 2
    odd = iota((8, 128), 1) % 2 == 1
    def station(s, acc):
        here = pair == s
        out = []
        for h in range(2):
            for j in range(4):
                cells = v[pl.ds((c * STATIONS + h * 64 + s) * CY + 8 * j, 8), :]
                out.append(jnp.where(here, pltpu.roll(cells, 2 * s + 1, 1), acc[len(out)]))
        return tuple(out)

    packed = lax.fori_loop(0, 64, station, tuple(jnp.zeros((8, 128), F32) for _ in range(8)), unroll=64)
    for k in range(2):
        left, right = [], []
        for j in (2 * k, 2 * k + 1):
            mask = fluid[8 * j : 8 * j + 8, :]
            near, far = packed[j], packed[4 + j]
            right.append(jnp.where(odd, pltpu.roll(far, 1, 1), near) * mask[:, CZ - 1 : CZ])
            left.append(jnp.where(odd, far, pltpu.roll(near, 127, 1)) * mask[:, 0:1])
        rows = pl.ds(c * CY + 16 * k, 16)
        to_right[rows, :] = jnp.concatenate(right, axis=0).astype(BF16)
        to_left[rows, :] = jnp.concatenate(left, axis=0).astype(BF16)


def stencil_station(v, lo, hi, col, tables, stepped, rounded, st, s):
    ahead = lax.rem(st + 1, STATIONS)
    behind = lax.rem(st + STATIONS - 1, STATIONS)
    half = st // 64
    shift = 126 - 2 * lax.rem(st, 64)
    first_row = iota((8, 128), 0) == 0
    last_row = iota((8, 128), 0) == 7
    first_lane = iota((8, 128), 1) == 0
    last_lane = iota((8, 128), 1) == CZ - 1

    def cells(c, t, j):
        return v[pl.ds((c * STATIONS + t) * CY + 8 * j, 8), :]

    m = [[cells(c, st, j) * tables[pl.ds(8 * j, 8), :] for j in range(4)] for c in range(3)]
    minus = [[1.0 - m[c][j] for j in range(4)] for c in range(3)]
    plus = [[1.0 + m[c][j] for j in range(4)] for c in range(3)]
    for c in range(3):
        edge_lo = jnp.broadcast_to(lo[pl.ds(c * STATIONS + st, 1), :], (8, 128))
        edge_hi = jnp.broadcast_to(hi[pl.ds(c * STATIONS + st, 1), :], (8, 128))
        down = [edge_lo] + [pltpu.roll(m[c][j], 1, 0) for j in range(4)]
        up = [pltpu.roll(m[c][j], 7, 0) for j in range(4)] + [edge_hi]
        results = []
        for j in range(4):
            south = jnp.where(first_row, down[j], down[j + 1])
            north = jnp.where(last_row, up[j + 1], up[j])
            ends = pltpu.roll(col[pl.ds((c * 2 + half) * CY + 8 * j, 8), :], shift, 1)
            lower = jnp.where(first_lane, ends, pltpu.roll(m[c][j], 1, 1))
            upper = jnp.where(last_lane, ends, pltpu.roll(m[c][j], CZ - 1, 1))
            total = minus[0][j] * cells(c, ahead, j) + plus[0][j] * cells(c, behind, j)
            total = total + (minus[1][j] * north + plus[1][j] * south)
            total = total + (minus[2][j] * upper + plus[2][j] * lower)
            own = tables[pl.ds(64 + 8 * j, 8), :] if c < 2 else 4.0
            total = total + own * m[c][j]
            results.append(total * tables[pl.ds(32 + 8 * j, 8), :])
        for k in range(2):
            value = jnp.concatenate(results[2 * k : 2 * k + 2], axis=0).astype(BF16)
            stepped[pl.ds(pl.multiple_of((c * STATIONS + st) * CY + 16 * k, 16), 16), :] = value
            rounded[pl.ds((c * 16 + s) * CY + 16 * k, 16), :] = value.astype(F32)


def pool_slab(rounded, feat):
    residue = iota((8, 128), 1) % 4
    merged = [None] * 30

    def put(f, r, value, source):
        shift = (r - source) % 128
        value = pltpu.roll(value, shift, 1) if shift else value
        merged[f] = value if merged[f] is None else jnp.where(residue == r, value, merged[f])

    for r in range(4):
        sums = [[None] * 4 for _ in range(3)]
        products = [None] * 6
        for dx in range(4):
            for dy in range(4):
                q = (dx // 2) * 2 + dy // 2
                u = [rounded[pl.ds((c * 16 + 4 * r + dx) * CY + dy, 8, stride=4), :] for c in range(3)]
                for c in range(3):
                    sums[c][q] = u[c] if sums[c][q] is None else sums[c][q] + u[c]
                for k, (a, b) in enumerate(PAIRS):
                    value = u[a] * u[b]
                    products[k] = value if products[k] is None else products[k] + value
        means = []
        for c in range(3):
            point = None
            for q in range(4):
                two = sums[c][q] + pltpu.roll(sums[c][q], 127, 1)
                put(c * 8 + 2 * q, r, two, 0)
                put(c * 8 + 2 * q + 1, r, two, 2)
                point = two if point is None else point + two
            means.append((point + pltpu.roll(point, 126, 1)) * (1.0 / 64))
        for k, (a, b) in enumerate(PAIRS):
            two = products[k] + pltpu.roll(products[k], 127, 1)
            four = two + pltpu.roll(two, 126, 1)
            put(24 + k, r, four * (1.0 / 64) - means[a] * means[b], 0)
    for f in range(24):
        feat[pl.ds(8 * f, 8), :] = merged[f] * 0.125
    for f in range(24, 30):
        feat[pl.ds(8 * f, 8), :] = merged[f].astype(BF16).astype(F32)


def widen(table, lanes):
    return jnp.concatenate([table] * (lanes // 128), axis=1)


def lane_sum(value):
    total = value[:, 0:128]
    for k in range(1, value.shape[1] // 128):
        total = total + value[:, 128 * k : 128 * k + 128]
    return total


def train_part(x, targets, win, wmid, wmid_t, wout, wout_t, bias_mid, bias_out, pred, g_in, g_mid, g_out, g_bmid, g_bout, g_loss):
    n = x.shape[1]
    h1 = jnp.dot(win[...], x, preferred_element_type=F32)
    t1 = jnp.tanh(h1)
    p1 = 1.0 + t1
    a1 = h1 * p1
    slope1 = p1 + a1 * (2.0 - p1)
    act1 = a1.astype(BF16)
    h2 = jnp.dot(wmid[...], act1, preferred_element_type=F32) + widen(bias_mid[...], n)
    p2 = 1.0 + jnp.tanh(h2)
    a2 = h2 * p2
    slope2 = p2 + a2 * (2.0 - p2)
    act2 = a2.astype(BF16)
    prediction = jnp.dot(wout[...], act2, preferred_element_type=F32)[0:8] + widen(bias_out[...], n)
    pred[...] = prediction
    residual = prediction - targets
    g_loss[...] += lane_sum(residual * residual)
    grad = (residual * (2.0 / (6 * SAMPLES))).astype(BF16).astype(F32)
    g_bout[...] += lane_sum(grad)
    grad = jnp.concatenate([grad, jnp.zeros_like(grad)], axis=0).astype(BF16)
    g_out[...] += lax.dot_general(grad, act2, NT, preferred_element_type=F32)
    d2 = jnp.dot(wout_t[...], grad, preferred_element_type=F32) * slope2
    g_bmid[...] += lane_sum(d2)
    grad2 = d2.astype(BF16)
    g_mid[...] += lax.dot_general(grad2, act1, NT, preferred_element_type=F32)
    d1 = jnp.dot(wmid_t[...], grad2, preferred_element_type=F32) * slope1
    grad1 = d1.astype(BF16)
    g_in[...] += lax.dot_general(grad1, x, NT, preferred_element_type=F32)


def keep_predictions(a, pred, tiles):
    lane = iota((8, 128), 1)
    point = lane % 64
    quarter = point // 4 % 4
    source = 4 * (point % 4) + point // 16
    low = lane < 64
    for b in range(2):
        blocks = [pred[:, 128 * (4 * b + q) : 128 * (4 * b + q) + 128] for q in range(4)]
        for c in range(8):
            index = source + 16 * c
            value = jnp.take_along_axis(blocks[0], index, axis=1)
            for q in range(1, 4):
                value = jnp.where(quarter == q, jnp.take_along_axis(blocks[q], index, axis=1), value)
            value = jnp.where(low, value, pltpu.roll(value, 5, 0))
            for k in range(3):
                tiles[pl.ds(k * TILES + a * 16 + b * 8 + c, 1), :] = value[k : k + 1]


def order_tiles(table, row, tiles, ordered):
    for a in range(8):
        for b in range(2):
            first = a * 16 + b * 8
            row[0:1, first : first + 8] = table[a, b : b + 1, :]
    place = iota((TILES, 128), 0)
    slot = place % N_GY * N_GZ + place // N_GY
    chosen = jnp.where(jnp.broadcast_to(row[0:1, :], (TILES, 128)) == slot, 1.0, 0.0).astype(BF16)
    for k in range(3):
        value = tiles[pl.ds(k * TILES, TILES), :]
        high = value.astype(BF16)
        rest = value - high.astype(F32)
        middle = rest.astype(BF16)
        last = (rest - middle.astype(F32)).astype(BF16)
        total = jnp.dot(chosen, high, preferred_element_type=F32)
        total = total + jnp.dot(chosen, middle, preferred_element_type=F32)
        total = total + jnp.dot(chosen, last, preferred_element_type=F32)
        ordered[:, k, :] = total


def pack_gradients(g_in, g_mid, g_out, g_bmid, g_bout, g_loss, tmp, grads):
    for t in range(64):
        grads[t // 5, t % 5] = g_mid[pl.ds(8 * (t // 2), 8), 128 * (t % 2) : 128 * (t % 2) + 128]
    tmp[:, 0:32] = g_in[...]
    for h in range(2):
        turned = jnp.transpose(tmp[pl.ds(128 * h, 128), :])
        for k in range(4):
            t = 64 + 2 * k + h
            grads[t // 5, t % 5] = turned[8 * k : 8 * k + 8]
    row = iota((8, 128), 0)
    lane = iota((8, 128), 1)
    sums_out = jnp.sum(g_bout[...], axis=1, keepdims=True)
    last = jnp.sum(jnp.where((lane == row + 8) & (row < 6), sums_out, 0.0), axis=0, keepdims=True)
    loss = jnp.sum(jnp.sum(g_loss[...], axis=1, keepdims=True), axis=0, keepdims=True)
    last = jnp.where(lane[0:1] == 0, loss, last)
    for k in range(2):
        t = 72 + k
        bias = jnp.sum(jnp.transpose(g_bmid[pl.ds(128 * k, 128), :]), axis=0, keepdims=True)
        value = g_out[pl.ds(0, 8), 128 * k : 128 * k + 128]
        grads[t // 5, t % 5] = jnp.where(row == 6, bias, jnp.where(row == 7, last, value))
    for t in range(74, 80):
        grads[t // 5, t % 5] = jnp.zeros((8, 128), F32)


def whole_kernel(
    vel, wall_any, hart_any, table_any, w_in_any, b_in_any, w_mid_any, b_mid_any, w_out_any, b_out_any,
    stepped_out, total, got,
    v, wall, hart, table, w_in, b_in, w_mid, b_mid, w_out, b_out,
    win, wmid, wmid_t, wout, wout_t, bias_mid, bias_out, tmp, row,
    edge_lo, edge_hi, to_left, to_right, got_lo, got_hi, got_left, got_right, lo, hi, col,
    stepped, rounded, tables, feat, xs, targets, pred, tiles, ordered,
    g_in, g_mid, g_out, g_bmid, g_bout, g_loss, grads, part, mine, column, hop,
    load, send_halo, recv_halo, store, s0, r0, s1, r1, s2, r2, s3, r3, s4, r4,
):
    y = lax.axis_index("gy")
    z = lax.axis_index("gz")
    slabs = [pl.ds(c * STATIONS * CY, STATIONS * CY) for c in range(3)]
    loads = [pltpu.make_async_copy(wall_any, wall, load.at[0])]
    loads += [pltpu.make_async_copy(vel.at[slabs[c]], v.at[slabs[c]], load.at[1 + c]) for c in range(3)]
    pairs = (
        (w_in_any, w_in), (b_in_any, b_in), (w_mid_any, w_mid), (b_mid_any, b_mid),
        (w_out_any, w_out), (b_out_any, b_out), (hart_any, hart), (table_any, table),
    )
    loads += [pltpu.make_async_copy(src, dst, load.at[4 + k]) for k, (src, dst) in enumerate(pairs)]
    for copy in loads:
        copy.start()

    barrier = pltpu.get_barrier_semaphore()
    for d in range(1, N_GY):
        pl.semaphore_signal(barrier, inc=1, device_id=((y + d) % N_GY, z), device_id_type=MESH)
    for d in range(1, N_GZ):
        pl.semaphore_signal(barrier, inc=1, device_id=(y, (z + d) % N_GZ), device_id_type=MESH)

    loads[0].wait()
    fluid = (1 - wall[...]).astype(F32)
    tables[pl.ds(0, 32), :] = fluid
    tables[pl.ds(32, 32), :] = fluid * 0.1
    for c in range(3):
        loads[1 + c].wait()
        pack_columns(v, tables, to_left, to_right, c)
        pack_edges(v, tables, edge_lo, edge_hi, c)
    pl.semaphore_wait(barrier, N_GY + N_GZ - 2)
    below = ((y + N_GY - 1) % N_GY, z)
    above = ((y + 1) % N_GY, z)
    left = (y, (z + N_GZ - 1) % N_GZ)
    right = (y, (z + 1) % N_GZ)
    copies = []
    for k, (src, dst, peer) in enumerate(
        ((to_left, got_right, left), (to_right, got_left, right), (edge_lo, got_hi, below), (edge_hi, got_lo, above))
    ):
        copy = pltpu.make_async_remote_copy(
            src, dst, send_halo.at[k], recv_halo.at[k], device_id=peer, device_id_type=MESH
        )
        copy.start()
        copies.append(copy)
    for copy in loads[4:]:
        copy.wait()
    tables[pl.ds(64, 32), :] = 2.0 - 2.0 * hart[...].astype(F32)
    prepare_weights(w_in, b_in, w_mid, b_mid, w_out, b_out, win, wmid, wmid_t, wout, wout_t, bias_mid, bias_out, tmp)
    for ref in (g_in, g_mid, g_out, g_bmid, g_bout, g_loss):
        ref[...] = jnp.zeros_like(ref)
    feat[pl.ds(240, 16), :] = jnp.ones((16, 128), F32)
    for copy in copies:
        copy.wait_recv()
    lo[...] = got_lo[...].astype(F32) * jnp.where(y > 0, 1.0, 0.0)
    hi[...] = got_hi[...].astype(F32) * jnp.where(y < N_GY - 1, 1.0, 0.0)
    has_left = jnp.where(z > 0, 1.0, 0.0)
    has_right = jnp.where(z < N_GZ - 1, 1.0, 0.0)
    odd = iota((16, 128), 1) % 2 == 1
    for c in range(3):
        for k in range(2):
            rows = pl.ds(c * CY + 16 * k, 16)
            lower = got_left[rows, :].astype(F32) * has_left
            upper = got_right[rows, :].astype(F32) * has_right
            near = jnp.where(odd, pltpu.roll(upper, 1, 1), pltpu.roll(lower, 2, 1))
            far = jnp.where(odd, upper, pltpu.roll(lower, 1, 1))
            col[pl.ds((c * 2) * CY + 16 * k, 16), :] = near
            col[pl.ds((c * 2 + 1) * CY + 16 * k, 16), :] = far

    def store_copy(c, a):
        rows = pl.ds(pl.multiple_of(c * STATIONS * CY + a * 16 * CY, 16), 16 * CY)
        return pltpu.make_async_copy(stepped.at[rows], stepped_out.at[rows], store.at[c])

    def stencil_slab(a, unroll):
        def station(s, inner):
            stencil_station(v, lo, hi, col, tables, stepped, rounded, a * 16 + s, s)
            return inner

        lax.fori_loop(0, 16, station, 0, unroll=unroll)
        for c in range(3):
            store_copy(c, a).start()

    def samples():
        pool_slab(rounded, feat)
        for yp in range(8):
            lanes = slice(128 * yp, 128 * yp + 128)
            xs[:, lanes] = feat[pl.ds(yp, 32, stride=8), :].astype(BF16)
            targets[:, lanes] = feat[pl.ds(192 + yp, 8, stride=8), :]

    def train(a):
        train_part(
            xs[...], targets[...], win, wmid, wmid_t, wout, wout_t, bias_mid, bias_out,
            pred, g_in, g_mid, g_out, g_bmid, g_bout, g_loss,
        )
        keep_predictions(a, pred, tiles)

    def slab(a, carry):
        samples()
        train(a)
        stencil_slab(a + 1, 16)
        return carry

    stencil_slab(0, 16)
    lax.fori_loop(0, SLABS - 1, slab, 0)
    samples()
    train(SLABS - 1)
    pack_gradients(g_in, g_mid, g_out, g_bmid, g_bout, g_loss, tmp, grads)

    def send(src, dst, ss, rs, qy, qz):
        pltpu.make_async_remote_copy(src, dst, ss, rs, device_id=(qy, qz), device_id_type=MESH).start()

    for d in range(1, N_GY):
        q = (y + d) % N_GY
        send(grads.at[q], part.at[y], s0, r0, q, z)
    order_tiles(table, row, tiles, ordered)
    for d in range(1, N_GZ):
        q = (z + d) % N_GZ
        send(ordered.at[pl.ds(q * N_GY, N_GY)], hop.at[z], s1, r1, y, q)
    hop[z] = ordered[pl.ds(z * N_GY, N_GY)]
    part[y] = grads[y]
    wait_bytes(part.at[pl.ds(0, N_GY - 1)], r0)
    column[z] = jnp.sum(part[...], axis=0)
    for d in range(1, N_GZ):
        q = (z + d) % N_GZ
        send(column.at[z], column.at[z], s2, r2, y, q)
    wait_bytes(hop.at[pl.ds(0, N_GZ - 1)], r1)
    for d in range(1, N_GY):
        q = (y + d) % N_GY
        send(hop.at[:, q], got.at[y], s3, r3, q, z)
    got[y] = hop[:, y]
    wait_bytes(column.at[pl.ds(0, N_GZ - 1)], r2)
    mine[...] = jnp.sum(column[...], axis=0)
    for d in range(1, N_GY):
        q = (y + d) % N_GY
        send(mine, total.at[y], s4, r4, q, z)
    total[y] = mine[...]
    for c in range(3):
        wait_bytes(stepped.at[slabs[c]], store.at[c])
    for copy in copies:
        copy.wait_send()
    wait_bytes(got.at[pl.ds(0, N_GY - 1)], r3)
    wait_bytes(total.at[pl.ds(0, N_GY - 1)], r4)
    wait_bytes(part.at[pl.ds(0, N_GY - 1)], s0)
    wait_bytes(hop.at[pl.ds(0, N_GZ - 1)], s1)
    wait_bytes(column.at[pl.ds(0, N_GZ - 1)], s2)
    wait_bytes(got.at[pl.ds(0, N_GY - 1)], s3)
    wait_bytes(total.at[pl.ds(0, N_GY - 1)], s4)


def whole_call(*arrays):
    vm = pl.BlockSpec(memory_space=pltpu.VMEM)
    anywhere = pl.BlockSpec(memory_space=pl.ANY)
    i32 = jnp.int32
    scratch = [
        ((ROWS, 128), F32), ((CY, 128), i32), ((CY, 128), i32), ((8, 2, 8), i32), ((24, HID), BF16), ((1, HID), F32),
        ((HID, HID), BF16), ((1, HID), F32), ((6, HID), BF16), ((1, 6), F32),
        ((HID, 32), BF16), ((HID, HID), BF16), ((HID, HID), BF16), ((16, HID), BF16), ((HID, 16), BF16),
        ((HID, 128), F32), ((8, 128), F32), ((HID, 128), F32), ((8, 128), i32),
        ((384, 128), BF16), ((384, 128), BF16), ((96, 128), BF16), ((96, 128), BF16),
        ((384, 128), BF16), ((384, 128), BF16), ((96, 128), BF16), ((96, 128), BF16),
        ((384, 128), F32), ((384, 128), F32), ((192, 128), F32),
        ((ROWS, 128), BF16), ((3 * 16 * CY, 128), F32), ((96, 128), F32), ((256, 128), F32),
        ((32, LANES), BF16), ((8, LANES), F32), ((8, LANES), F32), ((3 * TILES, 128), F32), ((TILES, 3, 128), F32),
        ((HID, 32), F32), ((HID, HID), F32), ((16, HID), F32), ((HID, 128), F32), ((8, 128), F32), ((8, 128), F32),
        ((N_GY, 5, 8, 128), F32), ((N_GY, 5, 8, 128), F32), ((5, 8, 128), F32), ((N_GZ, 5, 8, 128), F32),
        ((N_GZ, N_GY, 3, 128), F32),
    ]
    dma = pltpu.SemaphoreType.DMA
    return pl.pallas_call(
        whole_kernel,
        name="whole",
        out_shape=[
            jax.ShapeDtypeStruct((ROWS, 128), BF16),
            jax.ShapeDtypeStruct((N_GY, 5, 8, 128), F32),
            jax.ShapeDtypeStruct((N_GY, N_GZ, 3, 128), F32),
        ],
        in_specs=[anywhere] * 10,
        out_specs=[anywhere, vm, vm],
        scratch_shapes=[pltpu.VMEM(shape, kind) for shape, kind in scratch] + [dma((12,)), dma((4,)), dma((4,)), dma((3,))] + [dma] * 10,
        compiler_params=pltpu.CompilerParams(collective_id=0, has_side_effects=True, vmem_limit_bytes=VMEM_LIMIT << 20),
    )(*arrays)


def finish_kernel(
    stepped_any, total_any, got_any,
    stepped_out, pred_out, loss_out, in_out, bin_out, mid_out, bmid_out, out_out, bout_out,
    held, total, got, load, take, give,
):
    fetch_got = pltpu.make_async_copy(got_any, got, load.at[0])
    fetch_total = pltpu.make_async_copy(total_any, total, load.at[1])
    fetch_got.start()
    fetch_total.start()
    count = ROWS // MOVES
    parts = [pl.ds(k * count, count) for k in range(MOVES)]
    takes = [pltpu.make_async_copy(stepped_any.at[parts[k]], held.at[parts[k]], take.at[k]) for k in range(MOVES)]
    gives = [pltpu.make_async_copy(held.at[parts[k]], stepped_out.at[parts[k]], give.at[k]) for k in range(MOVES)]
    for copy in takes:
        copy.start()
    for k in range(MOVES):
        takes[k].wait()
        gives[k].start()
    fetch_got.wait()
    low = iota((3, 128), 1) < 64
    for j in range(TILES // 2):
        first = got[(2 * j) // N_GZ, (2 * j) % N_GZ]
        second = got[(2 * j + 1) // N_GZ, (2 * j + 1) % N_GZ]
        lanes = slice(128 * j, 128 * j + 128)
        pred_out[0:3, lanes] = jnp.where(low, first, pltpu.roll(second, 64, 1))
        pred_out[3:6, lanes] = jnp.where(low, pltpu.roll(first, 64, 1), second)
    fetch_total.wait()
    for t in range(64):
        mid_out[pl.ds(8 * (t // 2), 8), 128 * (t % 2) : 128 * (t % 2) + 128] = total[t // 5, t % 5]
    for h in range(2):
        lanes = slice(128 * h, 128 * h + 128)
        for k in range(4):
            t = 64 + 2 * k + h
            if k < 3:
                in_out[pl.ds(8 * k, 8), lanes] = total[t // 5, t % 5]
            else:
                bin_out[:, lanes] = total[t // 5, t % 5][6:7]
        last = total[(72 + h) // 5, (72 + h) % 5]
        out_out[:, lanes] = last[0:6]
        bmid_out[:, lanes] = last[6:7]
        if h == 0:
            loss_out[...] = last[7:8, 0:1] * (1.0 / (6 * SAMPLES))
            bout_out[...] = pltpu.roll(last, 120, 1)[7:8, 0:6]
    for copy in gives:
        copy.wait()


def finish_call(stepped, total, got):
    anywhere = pl.BlockSpec(memory_space=pl.ANY)
    vm = pl.BlockSpec(memory_space=pltpu.VMEM)
    return pl.pallas_call(
        finish_kernel,
        name="finish",
        out_shape=[
            jax.ShapeDtypeStruct((ROWS, 128), BF16),
            jax.ShapeDtypeStruct((6, 64 * 128), F32),
            jax.ShapeDtypeStruct((1, 1), F32),
            jax.ShapeDtypeStruct((24, HID), F32),
            jax.ShapeDtypeStruct((1, HID), F32),
            jax.ShapeDtypeStruct((HID, HID), F32),
            jax.ShapeDtypeStruct((1, HID), F32),
            jax.ShapeDtypeStruct((6, HID), F32),
            jax.ShapeDtypeStruct((1, 6), F32),
        ],
        in_specs=[anywhere] * 3,
        out_specs=[anywhere] + [vm] * 8,
        scratch_shapes=[
            pltpu.VMEM((ROWS, 128), BF16),
            pltpu.VMEM((N_GY, 5, 8, 128), F32),
            pltpu.VMEM((N_GY, N_GZ, 3, 128), F32),
            pltpu.SemaphoreType.DMA((2,)),
            pltpu.SemaphoreType.DMA((MOVES,)),
            pltpu.SemaphoreType.DMA((MOVES,)),
        ],
        compiler_params=pltpu.CompilerParams(vmem_limit_bytes=VMEM_LIMIT << 20),
    )(stepped, total, got)


def on_device(velocity, wall_mask, hartmann_mask, tile_table, w_in, b_in, w_mid, b_mid, w_out, b_out):
    stepped, total, got = whole_call(
        velocity.reshape(ROWS, CZ), wall_mask, hartmann_mask, tile_table,
        w_in.T, b_in.reshape(1, HID), w_mid, b_mid.reshape(1, HID), w_out, b_out.reshape(1, 6),
    )
    stepped, prediction, loss, grad_in, grad_bin, grad_mid, grad_bmid, grad_out, grad_bout = finish_call(stepped, total, got)
    return (
        stepped.reshape(3, STATIONS, CY, CZ),
        prediction,
        loss.reshape(()),
        grad_in.T,
        grad_bin.reshape(HID),
        grad_mid,
        grad_bmid.reshape(HID),
        grad_out,
        grad_bout.reshape(6),
    )


def solution(mesh):
    whole = P()
    in_specs = (P(None, None, "gy", "gz"), P("gy", "gz"), P("gy", "gz"), P(None, "gy", "gz")) + (whole,) * 6
    out_specs = (P(None, None, "gy", "gz"), P(None, ("gy", "gz"))) + (whole,) * 7
    return jax.shard_map(on_device, mesh=mesh, in_specs=in_specs, out_specs=out_specs, check_vma=False)
```

```python
import functools

import jax
import jax.numpy as jnp
from jax import lax
from jax.experimental import pallas as pl
from jax.experimental.pallas import tpu as pltpu
from jax.sharding import PartitionSpec as P

MESH = pl.DeviceIdType.MESH
STATIONS = 128
CY = 32
CZ = 128
HID = 256
N_GY = 16
N_GZ = 8
TILES = 128
SAMPLES = 1048576
ROWS = 3 * STATIONS * CY
SLABS = 8
VMEM_LIMIT = 56
FAR_GY = (8, 7, 9, 6, 10, 5, 11, 4, 12, 3, 13, 2, 14, 1, 15)
FAR_GZ = (4, 3, 5, 2, 6, 1, 7)
MOVES = 4
LANES = 1024
F32 = jnp.float32
BF16 = jnp.bfloat16
PAIRS = ((0, 0), (1, 1), (2, 2), (0, 1), (0, 2), (1, 2))
NT = (((1,), (1,)), ((), ()))


def iota(shape, dim):
    return lax.broadcasted_iota(jnp.int32, shape, dim)


def wait_bytes(ref, sem):
    pltpu.make_async_copy(ref, ref, sem).wait()


def column_table(row):
    wide = jnp.broadcast_to(row, (128, HID))
    return jnp.concatenate([jnp.transpose(wide[:, :128]), jnp.transpose(wide[:, 128:])], axis=0)


def prepare_weights(w_in, b_in, w_mid, b_mid, w_out, b_out, win, wmid, wmid_t, wout, wout_t, bias_mid, bias_out, tmp):
    lane = iota((HID, 128), 1)
    bias = column_table(b_in[...]) * 0.5
    high = bias.astype(BF16).astype(F32)
    tmp[pl.ds(0, 128), :] = jnp.zeros((128, 128), F32)
    halves = []
    for h in range(2):
        tmp[pl.ds(0, 24), :] = w_in[:, 128 * h : 128 * h + 128].astype(F32) * 0.5
        halves.append(jnp.transpose(tmp[pl.ds(0, 128), :]))
    full = jnp.concatenate(halves, axis=0)
    full = jnp.where(lane == 30, high, jnp.where(lane == 31, bias - high, full))
    win[...] = full[:, 0:32].astype(BF16)
    mid = w_mid[...].astype(F32) * 0.5
    wmid[...] = mid.astype(BF16)
    wmid_t[...] = jnp.transpose(mid).astype(BF16)
    bias_mid[...] = column_table(b_mid[...]) * 0.5
    for h in range(2):
        tmp[pl.ds(0, 128), :] = jnp.zeros((128, 128), F32)
        tmp[pl.ds(0, 6), :] = w_out[:, 128 * h : 128 * h + 128].astype(F32)
        wout[:, 128 * h : 128 * h + 128] = tmp[pl.ds(0, 16), :].astype(BF16)
        wout_t[pl.ds(128 * h, 128), :] = (jnp.transpose(tmp[pl.ds(0, 128), :])[:, 0:16] * 0.5).astype(BF16)
    row = iota((8, 128), 0)
    table = jnp.where(row >= 6, 1.0, 0.0)
    tmp[pl.ds(0, 1), 0:6] = b_out[...]
    wide = jnp.broadcast_to(tmp[pl.ds(0, 1), :], (128, 128))
    bias_out[...] = jnp.where(row < 6, jnp.transpose(wide)[0:8], table)


def pack_edges(v, fluid, edge_lo, edge_hi, c):
    first = c * STATIONS * CY
    rows = pl.ds(c * STATIONS, STATIONS)
    edge_lo[rows, :] = (v[pl.ds(first, STATIONS, stride=CY), :] * fluid[0:1, :]).astype(BF16)
    edge_hi[rows, :] = (v[pl.ds(first + CY - 1, STATIONS, stride=CY), :] * fluid[CY - 1 : CY, :]).astype(BF16)


def pack_columns(v, fluid, to_left, to_right, c):
    pair = iota((8, 128), 1) // 2
    odd = iota((8, 128), 1) % 2 == 1
    def station(s, acc):
        here = pair == s
        out = []
        for h in range(2):
            for j in range(4):
                cells = v[pl.ds((c * STATIONS + h * 64 + s) * CY + 8 * j, 8), :]
                out.append(jnp.where(here, pltpu.roll(cells, 2 * s + 1, 1), acc[len(out)]))
        return tuple(out)

    packed = lax.fori_loop(0, 64, station, tuple(jnp.zeros((8, 128), F32) for _ in range(8)), unroll=64)
    for k in range(2):
        left, right = [], []
        for j in (2 * k, 2 * k + 1):
            mask = fluid[8 * j : 8 * j + 8, :]
            near, far = packed[j], packed[4 + j]
            right.append(jnp.where(odd, pltpu.roll(far, 1, 1), near) * mask[:, CZ - 1 : CZ])
            left.append(jnp.where(odd, far, pltpu.roll(near, 127, 1)) * mask[:, 0:1])
        rows = pl.ds(c * CY + 16 * k, 16)
        to_right[rows, :] = jnp.concatenate(right, axis=0).astype(BF16)
        to_left[rows, :] = jnp.concatenate(left, axis=0).astype(BF16)


def stencil_station(v, lo, hi, col, tables, stepped, rounded, st, s):
    ahead = lax.rem(st + 1, STATIONS)
    behind = lax.rem(st + STATIONS - 1, STATIONS)
    half = st // 64
    shift = 126 - 2 * lax.rem(st, 64)
    first_row = iota((8, 128), 0) == 0
    last_row = iota((8, 128), 0) == 7
    first_lane = iota((8, 128), 1) == 0
    last_lane = iota((8, 128), 1) == CZ - 1

    def cells(c, t, j):
        return v[pl.ds((c * STATIONS + t) * CY + 8 * j, 8), :]

    m = [[cells(c, st, j) * tables[pl.ds(8 * j, 8), :] for j in range(4)] for c in range(3)]
    minus = [[1.0 - m[c][j] for j in range(4)] for c in range(3)]
    plus = [[1.0 + m[c][j] for j in range(4)] for c in range(3)]
    for c in range(3):
        edge_lo = jnp.broadcast_to(lo[pl.ds(c * STATIONS + st, 1), :], (8, 128))
        edge_hi = jnp.broadcast_to(hi[pl.ds(c * STATIONS + st, 1), :], (8, 128))
        down = [edge_lo] + [pltpu.roll(m[c][j], 1, 0) for j in range(4)]
        up = [pltpu.roll(m[c][j], 7, 0) for j in range(4)] + [edge_hi]
        results = []
        for j in range(4):
            south = jnp.where(first_row, down[j], down[j + 1])
            north = jnp.where(last_row, up[j + 1], up[j])
            ends = pltpu.roll(col[pl.ds((c * 2 + half) * CY + 8 * j, 8), :], shift, 1)
            lower = jnp.where(first_lane, ends, pltpu.roll(m[c][j], 1, 1))
            upper = jnp.where(last_lane, ends, pltpu.roll(m[c][j], CZ - 1, 1))
            total = minus[0][j] * cells(c, ahead, j) + plus[0][j] * cells(c, behind, j)
            total = total + (minus[1][j] * north + plus[1][j] * south)
            total = total + (minus[2][j] * upper + plus[2][j] * lower)
            own = tables[pl.ds(64 + 8 * j, 8), :] if c < 2 else 4.0
            total = total + own * m[c][j]
            results.append(total * tables[pl.ds(32 + 8 * j, 8), :])
        for k in range(2):
            value = jnp.concatenate(results[2 * k : 2 * k + 2], axis=0).astype(BF16)
            stepped[pl.ds(pl.multiple_of((c * STATIONS + st) * CY + 16 * k, 16), 16), :] = value
            rounded[pl.ds((c * 16 + s) * CY + 16 * k, 16), :] = value.astype(F32)


def pool_slab(rounded, feat):
    residue = iota((8, 128), 1) % 4
    merged = [None] * 30

    def put(f, r, value, source):
        shift = (r - source) % 128
        value = pltpu.roll(value, shift, 1) if shift else value
        merged[f] = value if merged[f] is None else jnp.where(residue == r, value, merged[f])

    for r in range(4):
        sums = [[None] * 4 for _ in range(3)]
        products = [None] * 6
        for dx in range(4):
            for dy in range(4):
                q = (dx // 2) * 2 + dy // 2
                u = [rounded[pl.ds((c * 16 + 4 * r + dx) * CY + dy, 8, stride=4), :] for c in range(3)]
                for c in range(3):
                    sums[c][q] = u[c] if sums[c][q] is None else sums[c][q] + u[c]
                for k, (a, b) in enumerate(PAIRS):
                    value = u[a] * u[b]
                    products[k] = value if products[k] is None else products[k] + value
        means = []
        for c in range(3):
            point = None
            for q in range(4):
                two = sums[c][q] + pltpu.roll(sums[c][q], 127, 1)
                put(c * 8 + 2 * q, r, two, 0)
                put(c * 8 + 2 * q + 1, r, two, 2)
                point = two if point is None else point + two
            means.append((point + pltpu.roll(point, 126, 1)) * (1.0 / 64))
        for k, (a, b) in enumerate(PAIRS):
            two = products[k] + pltpu.roll(products[k], 127, 1)
            four = two + pltpu.roll(two, 126, 1)
            put(24 + k, r, four * (1.0 / 64) - means[a] * means[b], 0)
    for f in range(24):
        feat[pl.ds(8 * f, 8), :] = merged[f] * 0.125
    for f in range(24, 30):
        feat[pl.ds(8 * f, 8), :] = merged[f].astype(BF16).astype(F32)


def widen(table, lanes):
    return jnp.concatenate([table] * (lanes // 128), axis=1)


def lane_sum(value):
    total = value[:, 0:128]
    for k in range(1, value.shape[1] // 128):
        total = total + value[:, 128 * k : 128 * k + 128]
    return total


def train_part(x, targets, win, wmid, wmid_t, wout, wout_t, bias_mid, bias_out, pred, g_in, g_mid, g_out, g_bmid, g_bout, g_loss):
    n = x.shape[1]
    h1 = jnp.dot(win[...], x, preferred_element_type=F32)
    t1 = jnp.tanh(h1)
    p1 = 1.0 + t1
    a1 = h1 * p1
    slope1 = p1 + a1 * (2.0 - p1)
    act1 = a1.astype(BF16)
    h2 = jnp.dot(wmid[...], act1, preferred_element_type=F32) + widen(bias_mid[...], n)
    p2 = 1.0 + jnp.tanh(h2)
    a2 = h2 * p2
    slope2 = p2 + a2 * (2.0 - p2)
    act2 = a2.astype(BF16)
    prediction = jnp.dot(wout[...], act2, preferred_element_type=F32)[0:8] + widen(bias_out[...], n)
    pred[...] = prediction
    residual = prediction - targets
    g_loss[...] += lane_sum(residual * residual)
    grad = (residual * (2.0 / (6 * SAMPLES))).astype(BF16).astype(F32)
    g_bout[...] += lane_sum(grad)
    grad = jnp.concatenate([grad, jnp.zeros_like(grad)], axis=0).astype(BF16)
    g_out[...] += lax.dot_general(grad, act2, NT, preferred_element_type=F32)
    d2 = jnp.dot(wout_t[...], grad, preferred_element_type=F32) * slope2
    g_bmid[...] += lane_sum(d2)
    grad2 = d2.astype(BF16)
    g_mid[...] += lax.dot_general(grad2, act1, NT, preferred_element_type=F32)
    d1 = jnp.dot(wmid_t[...], grad2, preferred_element_type=F32) * slope1
    grad1 = d1.astype(BF16)
    g_in[...] += lax.dot_general(grad1, x, NT, preferred_element_type=F32)


def keep_predictions(a, pred, tiles):
    lane = iota((8, 128), 1)
    point = lane % 64
    quarter = point // 4 % 4
    source = 4 * (point % 4) + point // 16
    low = lane < 64
    for b in range(2):
        blocks = [pred[:, 128 * (4 * b + q) : 128 * (4 * b + q) + 128] for q in range(4)]
        for c in range(8):
            index = source + 16 * c
            value = jnp.take_along_axis(blocks[0], index, axis=1)
            for q in range(1, 4):
                value = jnp.where(quarter == q, jnp.take_along_axis(blocks[q], index, axis=1), value)
            value = jnp.where(low, value, pltpu.roll(value, 5, 0))
            for k in range(3):
                tiles[pl.ds(k * TILES + a * 16 + b * 8 + c, 1), :] = value[k : k + 1]


def order_tiles(table, row, tiles, ordered):
    for a in range(8):
        for b in range(2):
            first = a * 16 + b * 8
            row[0:1, first : first + 8] = table[a, b : b + 1, :]
    place = iota((TILES, 128), 0)
    slot = place % N_GY * N_GZ + place // N_GY
    chosen = jnp.where(jnp.broadcast_to(row[0:1, :], (TILES, 128)) == slot, 1.0, 0.0).astype(BF16)
    for k in range(3):
        value = tiles[pl.ds(k * TILES, TILES), :]
        high = value.astype(BF16)
        rest = value - high.astype(F32)
        middle = rest.astype(BF16)
        last = (rest - middle.astype(F32)).astype(BF16)
        total = jnp.dot(chosen, high, preferred_element_type=F32)
        total = total + jnp.dot(chosen, middle, preferred_element_type=F32)
        total = total + jnp.dot(chosen, last, preferred_element_type=F32)
        ordered[:, k, :] = total


def pack_gradients(g_in, g_mid, g_out, g_bmid, g_bout, g_loss, tmp, grads):
    for t in range(64):
        grads[t // 5, t % 5] = g_mid[pl.ds(8 * (t // 2), 8), 128 * (t % 2) : 128 * (t % 2) + 128]
    tmp[:, 0:32] = g_in[...]
    for h in range(2):
        turned = jnp.transpose(tmp[pl.ds(128 * h, 128), :])
        for k in range(4):
            t = 64 + 2 * k + h
            grads[t // 5, t % 5] = turned[8 * k : 8 * k + 8]
    row = iota((8, 128), 0)
    lane = iota((8, 128), 1)
    sums_out = jnp.sum(g_bout[...], axis=1, keepdims=True)
    last = jnp.sum(jnp.where((lane == row + 8) & (row < 6), sums_out, 0.0), axis=0, keepdims=True)
    loss = jnp.sum(jnp.sum(g_loss[...], axis=1, keepdims=True), axis=0, keepdims=True)
    last = jnp.where(lane[0:1] == 0, loss, last)
    for k in range(2):
        t = 72 + k
        bias = jnp.sum(jnp.transpose(g_bmid[pl.ds(128 * k, 128), :]), axis=0, keepdims=True)
        value = g_out[pl.ds(0, 8), 128 * k : 128 * k + 128]
        grads[t // 5, t % 5] = jnp.where(row == 6, bias, jnp.where(row == 7, last, value))
    for t in range(74, 80):
        grads[t // 5, t % 5] = jnp.zeros((8, 128), F32)


def whole_kernel(
    vel, wall_any, hart_any, table_any, w_in_any, b_in_any, w_mid_any, b_mid_any, w_out_any, b_out_any,
    stepped_out, total, got,
    v, wall, hart, table, w_in, b_in, w_mid, b_mid, w_out, b_out,
    win, wmid, wmid_t, wout, wout_t, bias_mid, bias_out, tmp, row,
    edge_lo, edge_hi, to_left, to_right, got_lo, got_hi, got_left, got_right, lo, hi, col,
    stepped, rounded, tables, feat, xs, targets, pred, tiles, ordered,
    g_in, g_mid, g_out, g_bmid, g_bout, g_loss, grads, part, mine, column, hop,
    load, send_halo, recv_halo, store, s0, r0, s1, r1, s2, r2, s3, r3, s4, r4,
):
    y = lax.axis_index("gy")
    z = lax.axis_index("gz")
    slabs = [pl.ds(c * STATIONS * CY, STATIONS * CY) for c in range(3)]
    loads = [pltpu.make_async_copy(wall_any, wall, load.at[0])]
    loads += [pltpu.make_async_copy(vel.at[slabs[c]], v.at[slabs[c]], load.at[1 + c]) for c in range(3)]
    pairs = (
        (w_in_any, w_in), (b_in_any, b_in), (w_mid_any, w_mid), (b_mid_any, b_mid),
        (w_out_any, w_out), (b_out_any, b_out), (hart_any, hart), (table_any, table),
    )
    loads += [pltpu.make_async_copy(src, dst, load.at[4 + k]) for k, (src, dst) in enumerate(pairs)]
    for copy in loads:
        copy.start()

    barrier = pltpu.get_barrier_semaphore()
    for d in range(1, N_GY):
        pl.semaphore_signal(barrier, inc=1, device_id=((y + d) % N_GY, z), device_id_type=MESH)
    for d in range(1, N_GZ):
        pl.semaphore_signal(barrier, inc=1, device_id=(y, (z + d) % N_GZ), device_id_type=MESH)

    loads[0].wait()
    fluid = (1 - wall[...]).astype(F32)
    tables[pl.ds(0, 32), :] = fluid
    tables[pl.ds(32, 32), :] = fluid * 0.1
    for c in range(3):
        loads[1 + c].wait()
        pack_columns(v, tables, to_left, to_right, c)
        pack_edges(v, tables, edge_lo, edge_hi, c)
    pl.semaphore_wait(barrier, N_GY + N_GZ - 2)
    below = ((y + N_GY - 1) % N_GY, z)
    above = ((y + 1) % N_GY, z)
    left = (y, (z + N_GZ - 1) % N_GZ)
    right = (y, (z + 1) % N_GZ)
    copies = []
    for k, (src, dst, peer) in enumerate(
        ((to_left, got_right, left), (to_right, got_left, right), (edge_lo, got_hi, below), (edge_hi, got_lo, above))
    ):
        copy = pltpu.make_async_remote_copy(
            src, dst, send_halo.at[k], recv_halo.at[k], device_id=peer, device_id_type=MESH
        )
        copy.start()
        copies.append(copy)
    for copy in loads[4:]:
        copy.wait()
    tables[pl.ds(64, 32), :] = 2.0 - 2.0 * hart[...].astype(F32)
    prepare_weights(w_in, b_in, w_mid, b_mid, w_out, b_out, win, wmid, wmid_t, wout, wout_t, bias_mid, bias_out, tmp)
    for ref in (g_in, g_mid, g_out, g_bmid, g_bout, g_loss):
        ref[...] = jnp.zeros_like(ref)
    feat[pl.ds(240, 16), :] = jnp.ones((16, 128), F32)
    for copy in copies:
        copy.wait_recv()
    lo[...] = got_lo[...].astype(F32) * jnp.where(y > 0, 1.0, 0.0)
    hi[...] = got_hi[...].astype(F32) * jnp.where(y < N_GY - 1, 1.0, 0.0)
    has_left = jnp.where(z > 0, 1.0, 0.0)
    has_right = jnp.where(z < N_GZ - 1, 1.0, 0.0)
    odd = iota((16, 128), 1) % 2 == 1
    for c in range(3):
        for k in range(2):
            rows = pl.ds(c * CY + 16 * k, 16)
            lower = got_left[rows, :].astype(F32) * has_left
            upper = got_right[rows, :].astype(F32) * has_right
            near = jnp.where(odd, pltpu.roll(upper, 1, 1), pltpu.roll(lower, 2, 1))
            far = jnp.where(odd, upper, pltpu.roll(lower, 1, 1))
            col[pl.ds((c * 2) * CY + 16 * k, 16), :] = near
            col[pl.ds((c * 2 + 1) * CY + 16 * k, 16), :] = far

    def store_copy(c, a):
        rows = pl.ds(pl.multiple_of(c * STATIONS * CY + a * 16 * CY, 16), 16 * CY)
        return pltpu.make_async_copy(stepped.at[rows], stepped_out.at[rows], store.at[c])

    def stencil_slab(a, unroll):
        def station(s, inner):
            stencil_station(v, lo, hi, col, tables, stepped, rounded, a * 16 + s, s)
            return inner

        lax.fori_loop(0, 16, station, 0, unroll=unroll)
        for c in range(3):
            store_copy(c, a).start()

    def samples():
        pool_slab(rounded, feat)
        for yp in range(8):
            lanes = slice(128 * yp, 128 * yp + 128)
            xs[:, lanes] = feat[pl.ds(yp, 32, stride=8), :].astype(BF16)
            targets[:, lanes] = feat[pl.ds(192 + yp, 8, stride=8), :]

    def train(a):
        train_part(
            xs[...], targets[...], win, wmid, wmid_t, wout, wout_t, bias_mid, bias_out,
            pred, g_in, g_mid, g_out, g_bmid, g_bout, g_loss,
        )
        keep_predictions(a, pred, tiles)

    def slab(a, carry):
        samples()
        train(a)
        stencil_slab(a + 1, 16)
        return carry

    stencil_slab(0, 16)
    lax.fori_loop(0, SLABS - 1, slab, 0)
    samples()
    train(SLABS - 1)
    pack_gradients(g_in, g_mid, g_out, g_bmid, g_bout, g_loss, tmp, grads)

    def send(src, dst, ss, rs, qy, qz):
        pltpu.make_async_remote_copy(src, dst, ss, rs, device_id=(qy, qz), device_id_type=MESH).start()

    for d in FAR_GY:
        q = (y + d) % N_GY
        send(grads.at[q], part.at[y], s0, r0, q, z)
    order_tiles(table, row, tiles, ordered)
    for d in FAR_GZ:
        q = (z + d) % N_GZ
        send(ordered.at[pl.ds(q * N_GY, N_GY)], hop.at[z], s1, r1, y, q)
    hop[z] = ordered[pl.ds(z * N_GY, N_GY)]
    part[y] = grads[y]
    wait_bytes(part.at[pl.ds(0, N_GY - 1)], r0)
    column[z] = jnp.sum(part[...], axis=0)
    for d in FAR_GZ:
        q = (z + d) % N_GZ
        send(column.at[z], column.at[z], s2, r2, y, q)
    wait_bytes(hop.at[pl.ds(0, N_GZ - 1)], r1)
    for d in FAR_GY:
        q = (y + d) % N_GY
        send(hop.at[:, q], got.at[y], s3, r3, q, z)
    got[y] = hop[:, y]
    wait_bytes(column.at[pl.ds(0, N_GZ - 1)], r2)
    mine[...] = jnp.sum(column[...], axis=0)
    for d in FAR_GY:
        q = (y + d) % N_GY
        send(mine, total.at[y], s4, r4, q, z)
    total[y] = mine[...]
    for c in range(3):
        wait_bytes(stepped.at[slabs[c]], store.at[c])
    for copy in copies:
        copy.wait_send()
    wait_bytes(got.at[pl.ds(0, N_GY - 1)], r3)
    wait_bytes(total.at[pl.ds(0, N_GY - 1)], r4)
    wait_bytes(part.at[pl.ds(0, N_GY - 1)], s0)
    wait_bytes(hop.at[pl.ds(0, N_GZ - 1)], s1)
    wait_bytes(column.at[pl.ds(0, N_GZ - 1)], s2)
    wait_bytes(got.at[pl.ds(0, N_GY - 1)], s3)
    wait_bytes(total.at[pl.ds(0, N_GY - 1)], s4)


def whole_call(*arrays):
    vm = pl.BlockSpec(memory_space=pltpu.VMEM)
    anywhere = pl.BlockSpec(memory_space=pl.ANY)
    i32 = jnp.int32
    scratch = [
        ((ROWS, 128), F32), ((CY, 128), i32), ((CY, 128), i32), ((8, 2, 8), i32), ((24, HID), BF16), ((1, HID), F32),
        ((HID, HID), BF16), ((1, HID), F32), ((6, HID), BF16), ((1, 6), F32),
        ((HID, 32), BF16), ((HID, HID), BF16), ((HID, HID), BF16), ((16, HID), BF16), ((HID, 16), BF16),
        ((HID, 128), F32), ((8, 128), F32), ((HID, 128), F32), ((8, 128), i32),
        ((384, 128), BF16), ((384, 128), BF16), ((96, 128), BF16), ((96, 128), BF16),
        ((384, 128), BF16), ((384, 128), BF16), ((96, 128), BF16), ((96, 128), BF16),
        ((384, 128), F32), ((384, 128), F32), ((192, 128), F32),
        ((ROWS, 128), BF16), ((3 * 16 * CY, 128), F32), ((96, 128), F32), ((256, 128), F32),
        ((32, LANES), BF16), ((8, LANES), F32), ((8, LANES), F32), ((3 * TILES, 128), F32), ((TILES, 3, 128), F32),
        ((HID, 32), F32), ((HID, HID), F32), ((16, HID), F32), ((HID, 128), F32), ((8, 128), F32), ((8, 128), F32),
        ((N_GY, 5, 8, 128), F32), ((N_GY, 5, 8, 128), F32), ((5, 8, 128), F32), ((N_GZ, 5, 8, 128), F32),
        ((N_GZ, N_GY, 3, 128), F32),
    ]
    dma = pltpu.SemaphoreType.DMA
    return pl.pallas_call(
        whole_kernel,
        name="whole",
        out_shape=[
            jax.ShapeDtypeStruct((ROWS, 128), BF16),
            jax.ShapeDtypeStruct((N_GY, 5, 8, 128), F32),
            jax.ShapeDtypeStruct((N_GY, N_GZ, 3, 128), F32),
        ],
        in_specs=[anywhere] * 10,
        out_specs=[anywhere, vm, vm],
        scratch_shapes=[pltpu.VMEM(shape, kind) for shape, kind in scratch] + [dma((12,)), dma((4,)), dma((4,)), dma((3,))] + [dma] * 10,
        compiler_params=pltpu.CompilerParams(collective_id=0, has_side_effects=True, vmem_limit_bytes=VMEM_LIMIT << 20),
    )(*arrays)


def finish_kernel(
    stepped_any, total_any, got_any,
    stepped_out, pred_out, loss_out, in_out, bin_out, mid_out, bmid_out, out_out, bout_out,
    held, total, got, load, take, give,
):
    fetch_got = pltpu.make_async_copy(got_any, got, load.at[0])
    fetch_total = pltpu.make_async_copy(total_any, total, load.at[1])
    fetch_got.start()
    fetch_total.start()
    count = ROWS // MOVES
    parts = [pl.ds(k * count, count) for k in range(MOVES)]
    takes = [pltpu.make_async_copy(stepped_any.at[parts[k]], held.at[parts[k]], take.at[k]) for k in range(MOVES)]
    gives = [pltpu.make_async_copy(held.at[parts[k]], stepped_out.at[parts[k]], give.at[k]) for k in range(MOVES)]
    for copy in takes:
        copy.start()
    for k in range(MOVES):
        takes[k].wait()
        gives[k].start()
    fetch_got.wait()
    low = iota((3, 128), 1) < 64
    for j in range(TILES // 2):
        first = got[(2 * j) // N_GZ, (2 * j) % N_GZ]
        second = got[(2 * j + 1) // N_GZ, (2 * j + 1) % N_GZ]
        lanes = slice(128 * j, 128 * j + 128)
        pred_out[0:3, lanes] = jnp.where(low, first, pltpu.roll(second, 64, 1))
        pred_out[3:6, lanes] = jnp.where(low, pltpu.roll(first, 64, 1), second)
    fetch_total.wait()
    for t in range(64):
        mid_out[pl.ds(8 * (t // 2), 8), 128 * (t % 2) : 128 * (t % 2) + 128] = total[t // 5, t % 5]
    for h in range(2):
        lanes = slice(128 * h, 128 * h + 128)
        for k in range(4):
            t = 64 + 2 * k + h
            if k < 3:
                in_out[pl.ds(8 * k, 8), lanes] = total[t // 5, t % 5]
            else:
                bin_out[:, lanes] = total[t // 5, t % 5][6:7]
        last = total[(72 + h) // 5, (72 + h) % 5]
        out_out[:, lanes] = last[0:6]
        bmid_out[:, lanes] = last[6:7]
        if h == 0:
            loss_out[...] = last[7:8, 0:1] * (1.0 / (6 * SAMPLES))
            bout_out[...] = pltpu.roll(last, 120, 1)[7:8, 0:6]
    for copy in gives:
        copy.wait()


def finish_call(stepped, total, got):
    anywhere = pl.BlockSpec(memory_space=pl.ANY)
    vm = pl.BlockSpec(memory_space=pltpu.VMEM)
    return pl.pallas_call(
        finish_kernel,
        name="finish",
        out_shape=[
            jax.ShapeDtypeStruct((ROWS, 128), BF16),
            jax.ShapeDtypeStruct((6, 64 * 128), F32),
            jax.ShapeDtypeStruct((1, 1), F32),
            jax.ShapeDtypeStruct((24, HID), F32),
            jax.ShapeDtypeStruct((1, HID), F32),
            jax.ShapeDtypeStruct((HID, HID), F32),
            jax.ShapeDtypeStruct((1, HID), F32),
            jax.ShapeDtypeStruct((6, HID), F32),
            jax.ShapeDtypeStruct((1, 6), F32),
        ],
        in_specs=[anywhere] * 3,
        out_specs=[anywhere] + [vm] * 8,
        scratch_shapes=[
            pltpu.VMEM((ROWS, 128), BF16),
            pltpu.VMEM((N_GY, 5, 8, 128), F32),
            pltpu.VMEM((N_GY, N_GZ, 3, 128), F32),
            pltpu.SemaphoreType.DMA((2,)),
            pltpu.SemaphoreType.DMA((MOVES,)),
            pltpu.SemaphoreType.DMA((MOVES,)),
        ],
        compiler_params=pltpu.CompilerParams(vmem_limit_bytes=VMEM_LIMIT << 20),
    )(stepped, total, got)


def on_device(velocity, wall_mask, hartmann_mask, tile_table, w_in, b_in, w_mid, b_mid, w_out, b_out):
    stepped, total, got = whole_call(
        velocity.reshape(ROWS, CZ), wall_mask, hartmann_mask, tile_table,
        w_in.T, b_in.reshape(1, HID), w_mid, b_mid.reshape(1, HID), w_out, b_out.reshape(1, 6),
    )
    stepped, prediction, loss, grad_in, grad_bin, grad_mid, grad_bmid, grad_out, grad_bout = finish_call(stepped, total, got)
    return (
        stepped.reshape(3, STATIONS, CY, CZ),
        prediction,
        loss.reshape(()),
        grad_in.T,
        grad_bin.reshape(HID),
        grad_mid,
        grad_bmid.reshape(HID),
        grad_out,
        grad_bout.reshape(6),
    )


def solution(mesh):
    whole = P()
    in_specs = (P(None, None, "gy", "gz"), P("gy", "gz"), P("gy", "gz"), P(None, "gy", "gz")) + (whole,) * 6
    out_specs = (P(None, None, "gy", "gz"), P(None, ("gy", "gz"))) + (whole,) * 7
    return jax.shard_map(on_device, mesh=mesh, in_specs=in_specs, out_specs=out_specs, check_vma=False)
```
